128 devices in a mesh: blk: 16 (over y, z_lo, core), head: 8 (over z_hi, x).
Axes of the slice: x: 4, y: 4, z: 4 (z_hi: 2, z_lo: 2; z = z_hi * 2 + z_lo), core: 2. Of those that a mesh axis runs over, the one named last changes fastest.
Arguments:
- queries: bfloat16 [10240, 1024], P(('blk', 'head')), may hold values from -96 to 96
- keys: bfloat16 [10240, 1024], P(('blk', 'head')), may hold values from -18 to 18
- values: bfloat16 [10240, 1024], P(('blk', 'head')), may hold values from -6 to 6
- out_grad: bfloat16 [10240, 1024], P(('blk', 'head')), may hold values from -6 to 6
- doc_ids: int32 [10240], P('blk'), may hold values from 0 to 63, never falling along the last dimension, each value on 1 to 7680 neighbouring positions
Outputs:
- grad_queries: bfloat16 [10240, 1024], P(('blk', 'head'))
- grad_keys: bfloat16 [10240, 1024], P(('blk', 'head'))
- grad_values: bfloat16 [10240, 1024], P(('blk', 'head'))
The draws below stay inside these ranges and needn't reach their ends.
Inputs may be any that keep to these rules, and one draw needn't show every extreme that they name: doc_ids never falls along the window; each document holds 1 to 7680 frames and one holds exactly 7680.
All inputs are finite; a program needn't handle non-finite values.
Results may differ from the reference program's by a relative error of at most 0.0085.
Values may be sent and summed in bfloat16 or wider, within the bound.
No kernel may reach another device: no remote copies, remote signals or barrier semaphores. Data moves between devices by JAX's collectives and lax.ppermute only.
A program may use at most 64 MiB of HBM per device.

```python
import math
import jax
import jax.numpy as jnp
import numpy as np
from jax import lax

H = 16
HD = 64
D = 1024
TOK_DEV = 80
TOKENS = 10240
DOCS = 64
LONGEST = 7680
N_HEAD = 8


def paired_rows(key):
    base_keys = 3.0 * jnp.clip(jax.random.normal(jax.random.fold_in(key, 21), (TOKENS, D), jnp.float32), -6.0, 6.0)
    base_queries = jnp.clip(jax.random.normal(jax.random.fold_in(key, 22), (TOKENS, D), jnp.float32), -6.0, 6.0)
    keys_out = base_keys
    queries_out = base_queries
    return (jnp.clip(queries_out, -96.0, 96.0), jnp.clip(keys_out, -18.0, 18.0))


def draw_queries(key, part):
    return paired_rows(key)[0].astype(jnp.bfloat16)


def draw_keys(key, part):
    return paired_rows(key)[1].astype(jnp.bfloat16)


def steps_of(own_key, dims, split, least, largest):
    loudness, own = 1.0, jax.random.fold_in(own_key, 6)
    for axis_at, blocks in split:
        heights = jnp.exp(jax.random.uniform(jax.random.fold_in(own, axis_at), (blocks,), jnp.float32, least / len(split), largest / len(split)))
        loudness = loudness * jnp.repeat(heights, dims[axis_at] // blocks).reshape([-1 if axis == axis_at else 1 for axis in range(len(dims))])
    return loudness


def split_up(count, total, most, skew):
    loads = [(1 << 20) // math.isqrt(standing ** skew) + 1 for standing in range(2, count + 1)]
    rest, counts = total - most - (count - 1), [1] * (count - 1)
    while rest > 0:
        free = [i for i in range(count - 1) if counts[i] < most]
        pool, remaining = sum([loads[i] for i in free]), rest
        for i in free:
            extra = min(most - counts[i], max(1, remaining * loads[i] // pool), rest)
            counts[i] = counts[i] + extra
            rest = rest - extra
    return np.array([most] + counts)


def uneven(key, count, total, bound, lean):
    if count == 2:
        one = jax.random.randint(key, (), max(1, total - bound), min(bound, total - 1) + 1)
        return jnp.stack([one, total - one])
    tallies = jnp.asarray(split_up(count, total, bound, lean), jnp.int32)
    couples = (count - 1) // 2
    donor, sink = tallies[1:1 + 2 * couples:2], tallies[2:2 + 2 * couples:2]
    margin = jnp.minimum(donor - 1, bound - sink)
    shifted = jax.random.randint(jax.random.fold_in(key, 1), (couples,), 0, 1 << 20) % (margin + 1)
    tallies = tallies.at[1:1 + 2 * couples:2].set(donor - shifted).at[2:2 + 2 * couples:2].set(sink + shifted)
    return tallies[jax.random.permutation(jax.random.fold_in(key, 2), count)]


def scatter_about(key, shape, scale, limit, pieces=(), held_as=jnp.bfloat16):
    factor_of = steps_of(key, shape, pieces, -0.22, 0.18) if pieces else 1.0
    result = jax.random.normal(key, shape, jnp.float32) * scale * factor_of
    return jnp.minimum(jnp.maximum(result, -limit), limit).astype(held_as)


def setup_inputs(seed: int = 0) -> dict:
    key_of = jax.random.split(jax.random.key(seed), 6)
    queries = draw_queries(jax.random.fold_in(key_of[5], 71), 0)
    keys = draw_keys(jax.random.fold_in(key_of[5], 71), 0)
    values = scatter_about(key_of[2], (TOKENS, D), 1.0, 6.0, ((0, 128),))
    out_grad = scatter_about(key_of[3], (TOKENS, D), 1.0, 6.0, ((0, 128),))
    doc_ids = jnp.searchsorted(jnp.cumsum(uneven(key_of[4], DOCS, TOKENS, LONGEST, 2)), jnp.arange(TOKENS), side="right").astype(jnp.int32)
    return dict(queries=queries, keys=keys, values=values, out_grad=out_grad, doc_ids=doc_ids)


masked_score = -1e+30

def head_backward(query_head, key_head, value_head, grad_head, doc_ids):
    block_rows = TOK_DEV * N_HEAD
    block_count = TOKENS // block_rows
    score_scale = 1.0 / math.sqrt(HD)
    query_blocks = query_head.reshape(block_count, block_rows, HD)
    grad_blocks = grad_head.reshape(block_count, block_rows, HD)
    doc_blocks = doc_ids.reshape(block_count, block_rows)

    def scores_of(query_part, grad_part, doc_part):
        scores = jnp.dot(query_part, key_head.T, precision=lax.Precision.HIGHEST, preferred_element_type=jnp.float32) * score_scale
        prob_grad = jnp.dot(grad_part, value_head.T, precision=lax.Precision.HIGHEST, preferred_element_type=jnp.float32)
        same_doc = doc_part[:, None] == doc_ids[None, :]
        return (scores, prob_grad, same_doc)

    def stats(operands):
        scores, prob_grad, same_doc = scores_of(operands[0], operands[1], operands[2])
        row_max = lax.optimization_barrier(jnp.max(jnp.where(same_doc, scores, masked_score), axis=1))
        weights = jnp.where(same_doc, jnp.exp(scores - row_max[:, None]), 0.0)
        row_total = lax.optimization_barrier(jnp.sum(weights, axis=1))
        return (row_max + jnp.log(row_total), lax.optimization_barrier(jnp.sum(weights * prob_grad, axis=1)) / row_total)
    log_total, row_dot = lax.map(stats, (query_blocks, grad_blocks, doc_blocks))

    def accumulate(totals, operands):
        grad_key, grad_value = totals
        query_part, grad_part, doc_part, total_part, dot_part = operands
        scores, prob_grad, same_doc = scores_of(query_part, grad_part, doc_part)
        probs = jnp.where(same_doc, jnp.exp(scores - total_part[:, None]), 0.0)
        rounded_probs = lax.optimization_barrier(probs.astype(jnp.bfloat16)).astype(jnp.float32)
        grad_value = grad_value + jnp.dot(rounded_probs.T, grad_part, precision=lax.Precision.HIGHEST, preferred_element_type=jnp.float32)
        score_grad = score_scale * probs * (prob_grad - dot_part[:, None])
        score_grad = lax.optimization_barrier(score_grad.astype(jnp.bfloat16)).astype(jnp.float32)
        grad_query = jnp.dot(score_grad, key_head, precision=lax.Precision.HIGHEST, preferred_element_type=jnp.float32)
        grad_key = grad_key + jnp.dot(score_grad.T, query_part, precision=lax.Precision.HIGHEST, preferred_element_type=jnp.float32)
        return ((grad_key, grad_value), grad_query)
    zero_rows = jnp.zeros((TOKENS, HD), jnp.float32)
    totals, grad_query = lax.scan(accumulate, (zero_rows, zero_rows), (query_blocks, grad_blocks, doc_blocks, log_total, row_dot))
    return (grad_query.reshape(TOKENS, HD), totals[0], totals[1])

def reference(queries, keys, values, out_grad, doc_ids):

    def by_heads(source):
        return source.astype(jnp.float32).reshape(TOKENS, H, HD).transpose(1, 0, 2)

    def per_head(operands):
        return head_backward(operands[0], operands[1], operands[2], operands[3], doc_ids)
    grad_query, grad_key, grad_value = lax.map(per_head, (by_heads(queries), by_heads(keys), by_heads(values), by_heads(out_grad)))

    def merged(source):
        return source.transpose(1, 0, 2).reshape(TOKENS, H * HD).astype(jnp.bfloat16)
    return (merged(grad_query), merged(grad_key), merged(grad_value))
```

```python
import functools
import math

import jax
import jax.numpy as jnp
from jax import lax
from jax.experimental import pallas as pl
from jax.experimental.pallas import tpu as pltpu
from jax.sharding import Mesh
from jax.sharding import PartitionSpec as P

BF = jnp.bfloat16
F32 = jnp.float32
HD = 64
HEADS = 16
ROWS = 80
LONG = 7680
NQ, NK = 5120, 2560
LQ, LK = LONG // 2, LONG // 4
RQ, RK = NQ - LQ, NK - LK
SCALE = 1.0 / math.sqrt(HD)
LOG2_SCALE = SCALE * math.log2(math.e)
NEG = -1e30
BLK = ("y", "zl", "c")
VMEM_LIMIT = 56 << 20


def dot_nt(a, b):
    return lax.dot_general(a, b, (((1,), (1,)), ((), ())), preferred_element_type=F32)


def dot_nn(a, b):
    return lax.dot_general(a, b, (((1,), (0,)), ((), ())), preferred_element_type=F32)


def lane_of(x):
    return lax.broadcasted_iota(jnp.int32, x.shape, x.ndim - 1)


def row_of(x):
    return lax.broadcasted_iota(jnp.int32, x.shape, 0)


def swap_halves(x):
    return pltpu.roll(x, HD, 1)


def vmem_call(kernel, out_shape, scratch=(), smem=0, n_in=0, flops=0, nbytes=0, name=None):
    vm = pl.BlockSpec(memory_space=pltpu.VMEM)
    sm = pl.BlockSpec(memory_space=pltpu.SMEM)
    return pl.pallas_call(
        kernel,
        out_shape=out_shape,
        in_specs=[sm] * smem + [vm] * n_in,
        out_specs=[vm] * len(out_shape),
        scratch_shapes=list(scratch),
        compiler_params=pltpu.CompilerParams(vmem_limit_bytes=VMEM_LIMIT),
        cost_estimate=pl.CostEstimate(flops=flops, bytes_accessed=nbytes, transcendentals=0),
        name=name,
    )


def pack_kernel(q_ref, k_ref, v_ref, g_ref, qg_ref, kv_ref):
    for pair in range(HEADS // 2):
        cols = slice(pair * 128, pair * 128 + 128)
        for a_ref, b_ref, out_ref, copies in ((q_ref, g_ref, qg_ref, 4), (k_ref, v_ref, kv_ref, 2)):
            a = a_ref[:, cols].astype(F32)
            b = b_ref[:, cols].astype(F32)
            low = lane_of(a) < HD
            even = jnp.where(low, a, swap_halves(b)).astype(BF)
            odd = jnp.where(low, swap_halves(a), b).astype(BF)
            for c in range(copies):
                out_ref[2 * pair * copies + c] = even
                out_ref[(2 * pair + 1) * copies + c] = odd


def gather_rows(src_ref, dst_ref, base, off, rows, main):
    def move(i, _):
        at = lax.rem(base + i * 16, rows)
        dst_ref[pl.ds(pl.multiple_of(i * 16, 16), 16), :] = src_ref[
            pl.ds(pl.multiple_of(at, 16), 16), :
        ]
        return 0

    lax.fori_loop(0, rows // 16, move, 0, unroll=8)
    first = dst_ref[0:16, :]
    last = dst_ref[main : main + 16, :]
    early = row_of(first) < off
    dst_ref[0:16, :] = jnp.where(early, last, first)
    dst_ref[main : main + 16, :] = jnp.where(early, first, last)


def halves(x):
    zero = jnp.zeros_like(x)
    low = lane_of(x) < HD
    return jnp.where(low, x, zero), jnp.where(low, zero, x)


def columns_of(doc_row):
    return jnp.broadcast_to(doc_row, (128, doc_row.shape[1])).T


def same_doc(doc_cols, doc_row):
    wide = jnp.concatenate([doc_cols] * (doc_row.shape[1] // 128), axis=1)
    return wide == doc_row


def totals_kernel(
    at_ref, qg_in, kv_in, qdoc_ref, kdoc_ref, lse_ref, dot_ref, qg_ref, kv_ref, kvt_ref, vet_ref, kcol_ref
):
    gather_rows(qg_in, qg_ref, at_ref[0], at_ref[1], NQ, LQ)
    gather_rows(kv_in, kv_ref, at_ref[2], at_ref[3], NK, LK)
    kvt = kv_ref[...].astype(F32).T
    kvt_ref[...] = kvt.astype(BF)
    vet_ref[...] = jnp.where(row_of(kvt) < HD, 1.0, kvt).astype(BF)
    kcol_ref[...] = columns_of(kdoc_ref[...])

    def tile(rows, width, keys, step, doc_row):
        qg = qg_ref[rows, :]
        q0, _ = halves(qg)
        starts = list(range(keys[0], keys[1], step))
        scores, tops, outs = {}, [], []

        def finish(at):
            s = scores.pop(at)
            mask = None
            if doc_row is not None:
                mask = same_doc(kcol_ref[at - LK : at - LK + step, :], doc_row)
                s = jnp.where(mask, s, NEG)
            top = jnp.max(s, axis=0, keepdims=True) * LOG2_SCALE
            p = jnp.exp2(s * LOG2_SCALE - top)
            if mask is not None:
                p = jnp.where(mask, p, 0.0)
            outs.append(dot_nn(vet_ref[:, at : at + step], p.astype(BF)))
            tops.append(top)

        for n, at in enumerate(starts):
            scores[at] = dot_nt(kv_ref[at : at + step, :], q0)
            if n:
                finish(starts[n - 1])
        finish(starts[-1])
        top = functools.reduce(jnp.maximum, tops)
        out = sum(o * jnp.exp2(t - top) for o, t in zip(outs, tops))
        total = out[0:1, :]
        grad_t = qg.astype(F32).T
        dot = jnp.sum(out[HD:, :] * grad_t[HD:, :], axis=0, keepdims=True)
        if doc_row is not None:
            empty = total <= 0.0
            total = jnp.where(empty, 1.0, total)
            top = jnp.where(empty, NEG, top)
        lse_ref[:, rows] = top + jnp.log2(total)
        dot_ref[:, rows] = dot / total

    wide = 768

    def long_tile(t, _):
        tile(pl.ds(pl.multiple_of(t * wide, wide), wide), wide, (0, LK), 384, None)
        return 0

    lax.fori_loop(0, LQ // wide, long_tile, 0)

    def rest_tile(t, _):
        rows = pl.ds(pl.multiple_of(LQ + t * 640, 128), 640)
        docs = qdoc_ref[:, pl.ds(pl.multiple_of(t * 640, 128), 640)]
        tile(rows, 640, (LK, NK), 320, docs)
        return 0

    lax.fori_loop(0, RQ // 640, rest_tile, 0)


def grads_kernel(
    at_ref, qg_ref, kv_ref, kvt_ref, qdoc_ref, kdoc_ref, s0, s1, s2, s3,
    dq_out, dkv_out, lse_ref, dot_ref, kcol_ref, dq_ref, dkv_ref,
):
    lses = [s[0:1, :] for s in (s0, s1, s2, s3)]
    dots = [s[1:2, :] for s in (s0, s1, s2, s3)]
    top = functools.reduce(jnp.maximum, lses)
    shares = [jnp.exp2(one - top) for one in lses]
    total = sum(shares)
    lse_ref[...] = top + jnp.log2(total)
    dot_ref[...] = sum(w * d for w, d in zip(shares, dots)) / total
    kcol_ref[...] = columns_of(kdoc_ref[...])
    dkv_ref[...] = jnp.zeros_like(dkv_ref)

    def tile(rows, keys, step, doc_row):
        q0, g0 = halves(qg_ref[rows, :])
        lse = lse_ref[:, rows]
        dot = dot_ref[:, rows]
        both = jnp.concatenate([g0, q0], axis=0)
        acc = None
        for at in range(keys[0], keys[1], step):
            kv = kv_ref[at : at + step, :]
            p = jnp.exp2(dot_nt(kv, q0) * LOG2_SCALE - lse)
            if doc_row is not None:
                p = jnp.where(same_doc(kcol_ref[at - LK : at - LK + step, :], doc_row), p, 0.0)
            ds = (p * (dot_nt(kv, g0) - dot)).astype(BF)
            dkv_ref[at : at + step, :] += dot_nn(jnp.concatenate([p.astype(BF), ds], axis=1), both)
            part = dot_nn(kvt_ref[0:HD, at : at + step], ds)
            acc = part if acc is None else acc + part
        acc = acc * SCALE
        dq_ref[rows, :] = jnp.concatenate([acc, acc], axis=0).T

    wide = 768

    def long_tile(t, _):
        tile(pl.ds(pl.multiple_of(t * wide, wide), wide), (0, LK), 384, None)
        return 0

    lax.fori_loop(0, LQ // wide, long_tile, 0)

    def rest_tile(t, _):
        rows = pl.ds(pl.multiple_of(LQ + t * 640, 128), 640)
        docs = qdoc_ref[:, pl.ds(pl.multiple_of(t * 640, 128), 640)]
        tile(rows, (LK, NK), 320, docs)
        return 0

    lax.fori_loop(0, RQ // 640, rest_tile, 0)

    def swap_back(ref, off, main):
        first = ref[0:16, :]
        last = ref[main : main + 16, :]
        early = row_of(first) < off
        ref[0:16, :] = jnp.where(early, last, first)
        ref[main : main + 16, :] = jnp.where(early, first, last)

    swap_back(dq_ref, at_ref[1], LQ)
    swap_back(dkv_ref, at_ref[3], LK)
    base_q, base_k = at_ref[0], at_ref[2]

    def sixteen(ref, at, base, rows):
        spot = lax.rem(at + rows - base, rows)
        return ref[pl.ds(pl.multiple_of(spot, 16), 16), :]

    def store_dq(c, _):
        groups = [sixteen(dq_ref, c * ROWS + 16 * n, base_q, NQ) for n in range(5)]
        low = lane_of(groups[0]) < HD
        dq_out[c, 0:16, :] = jnp.where(low, groups[0], groups[1]).astype(BF)
        dq_out[c, 16:32, :] = jnp.where(low, groups[2], groups[3]).astype(BF)
        dq_out[c, 32:48, :] = groups[4].astype(BF)
        return 0

    lax.fori_loop(0, NQ // ROWS, store_dq, 0, unroll=2)

    def store_dkv(c, _):
        for n in range(5):
            one = sixteen(dkv_ref, c * ROWS + 16 * n, base_k, NK)
            dkv_out[c, 16 * n : 16 * n + 16, :] = jnp.where(
                lane_of(one) < HD, one * SCALE, one
            ).astype(BF)
        return 0

    lax.fori_loop(0, NK // ROWS, store_dkv, 0, unroll=2)


def join_kernel(dq_ref, dkv_ref, q_out, k_out, v_out):
    for pair in range(HEADS // 2):
        cols = slice(pair * 128, pair * 128 + 128)
        even, odd = 2 * pair, 2 * pair + 1

        def total(ref, h, copies):
            return sum(ref[h * copies + c].astype(F32) for c in range(copies))

        a, b = total(dq_ref, even, 4), total(dq_ref, odd, 4)
        a_swap, b_swap = swap_halves(a), swap_halves(b)
        low = lane_of(a[0:16]) < HD
        for n in range(5):
            part = slice(16 * (n // 2), 16 * (n // 2) + 16)
            if n % 2 == 0:
                rows = jnp.where(low, a[part], b_swap[part])
            else:
                rows = jnp.where(low, a_swap[part], b[part])
            q_out[16 * n : 16 * n + 16, cols] = rows.astype(BF)
        a, b = total(dkv_ref, even, 2), total(dkv_ref, odd, 2)
        low = lane_of(a) < HD
        k_out[:, cols] = jnp.where(low, a, swap_halves(b)).astype(BF)
        v_out[:, cols] = jnp.where(low, swap_halves(a), b).astype(BF)


def doc_plan(docs, rows, main, long_doc):
    start = jnp.sum((docs < long_doc).astype(jnp.int32))
    off = lax.rem(start, 16)
    base = start - off
    turned = lax.dynamic_slice(jnp.concatenate([docs, docs]), (base,), (rows,))
    early = jnp.arange(16) < off
    rest = jnp.concatenate(
        [jnp.where(early, turned[:16], turned[main : main + 16]), turned[main + 16 :]]
    )
    return base, off, rest.astype(F32).reshape(1, rows - main)


def body(queries, keys, values, out_grad, doc_ids):
    shape = jax.ShapeDtypeStruct
    all_docs = lax.all_gather(doc_ids, BLK, axis=0, tiled=True)
    qg, kv = vmem_call(
        pack_kernel,
        [shape((64, ROWS, 128), BF), shape((32, ROWS, 128), BF)],
        n_in=4,
        name="pack",
    )(queries, keys, values, out_grad)
    kv = lax.all_to_all(kv, BLK + ("zh",), 0, 0, tiled=True).reshape(NK, 128)
    qg = lax.all_to_all(qg, BLK + ("x",), 0, 0, tiled=True).reshape(NQ, 128)

    docs = all_docs.reshape(16, 2, 4, ROWS)
    long_doc = all_docs[all_docs.shape[0] // 2]
    zh, x = lax.axis_index("zh"), lax.axis_index("x")
    q_docs = lax.dynamic_index_in_dim(docs, zh, 1, keepdims=False).reshape(NQ)
    k_docs = lax.dynamic_index_in_dim(docs, x, 2, keepdims=False).reshape(NK)
    base_q, off_q, rest_q = doc_plan(q_docs, NQ, LQ, long_doc)
    base_k, off_k, rest_k = doc_plan(k_docs, NK, LK, long_doc)
    at = jnp.stack([base_q, off_q, base_k, off_k])

    lse, dot, qg, kv, kvt = vmem_call(
        totals_kernel,
        [
            shape((1, NQ), F32),
            shape((1, NQ), F32),
            shape((NQ, 128), BF),
            shape((NK, 128), BF),
            shape((128, NK), BF),
        ],
        scratch=[pltpu.VMEM((128, NK), BF), pltpu.VMEM((RK, 128), F32)],
        smem=1,
        n_in=4,
        name="totals",
    )(at, qg, kv, rest_q, rest_k)
    stats = jnp.concatenate([lse, dot], axis=0)
    others = [
        lax.ppermute(stats, "x", [(i, (i + n) % 4) for i in range(4)]) for n in (1, 2, 3)
    ]
    dq, dkv = vmem_call(
        grads_kernel,
        [shape((64, 48, 128), BF), shape((32, ROWS, 128), BF)],
        scratch=[
            pltpu.VMEM((1, NQ), F32),
            pltpu.VMEM((1, NQ), F32),
            pltpu.VMEM((RK, 128), F32),
            pltpu.VMEM((NQ, 128), F32),
            pltpu.VMEM((NK, 128), F32),
        ],
        smem=1,
        n_in=9,
        name="grads",
    )(at, qg, kv, kvt, rest_q, rest_k, stats, *others)
    dkv = lax.all_to_all(dkv, BLK + ("zh",), 0, 0, tiled=True)
    dq = lax.all_to_all(dq, BLK + ("x",), 0, 0, tiled=True)
    return tuple(
        vmem_call(join_kernel, [shape((ROWS, HEADS * HD), BF)] * 3, n_in=2, name="join")(dq, dkv)
    )


def solution(mesh):
    fine = Mesh(mesh.devices.reshape(4, 2, 2, 2, 4), BLK + ("zh", "x"))
    rows = P(BLK + ("zh", "x"), None)
    return jax.shard_map(
        body,
        mesh=fine,
        in_specs=(rows, rows, rows, rows, P(BLK)),
        out_specs=(rows, rows, rows),
        check_vma=False,
    )
```

```python
import functools
import math

import jax
import jax.numpy as jnp
from jax import lax
from jax.experimental import pallas as pl
from jax.experimental.pallas import tpu as pltpu
from jax.sharding import Mesh
from jax.sharding import PartitionSpec as P

BF = jnp.bfloat16
F32 = jnp.float32
HD = 64
HEADS = 16
ROWS = 80
OWN = 1280
LONG = 960
REST = OWN - LONG
SENT = OWN + 16
STEP = 240
WIDE = 1408
SCALE = 1.0 / math.sqrt(HD)
LOG2_SCALE = SCALE * math.log2(math.e)
NEG = -1e30
BLK = ("y", "zl", "c")
VMEM_LIMIT = 24 << 20


def dot_nt(a, b):
    return lax.dot_general(a, b, (((1,), (1,)), ((), ())), preferred_element_type=F32)


def dot_nn(a, b):
    return lax.dot_general(a, b, (((1,), (0,)), ((), ())), preferred_element_type=F32)


def lane_of(x):
    return lax.broadcasted_iota(jnp.int32, x.shape, x.ndim - 1)


def row_of(x):
    return lax.broadcasted_iota(jnp.int32, x.shape, 0)


def swap_halves(x):
    return pltpu.roll(x, HD, 1)


def shape(*dims, dtype=BF):
    return jax.ShapeDtypeStruct(dims, dtype)


def call(kernel, name, outs, args, smem_in=0, smem_out=0, scratch=(), flops=1 << 20):
    vm = pl.BlockSpec(memory_space=pltpu.VMEM)
    sm = pl.BlockSpec(memory_space=pltpu.SMEM)
    return pl.pallas_call(
        kernel,
        out_shape=outs,
        in_specs=[sm] * smem_in + [vm] * (len(args) - smem_in),
        out_specs=[sm] * smem_out + [vm] * (len(outs) - smem_out),
        scratch_shapes=list(scratch),
        compiler_params=pltpu.CompilerParams(vmem_limit_bytes=VMEM_LIMIT),
        cost_estimate=pl.CostEstimate(flops=flops, bytes_accessed=1 << 20, transcendentals=0),
        name=name,
    )(*args)


def pack_kernel(q_ref, k_ref, v_ref, g_ref, doc_ref, out_ref):
    for pair in range(HEADS // 2):
        cols = slice(pair * 128, pair * 128 + 128)
        for a_ref, b_ref, at in ((q_ref, g_ref, 0), (k_ref, v_ref, ROWS)):
            a = a_ref[:, cols].astype(F32)
            b = b_ref[:, cols].astype(F32)
            low = lane_of(a) < HD
            out_ref[2 * pair, at : at + ROWS, :] = jnp.where(low, a, swap_halves(b)).astype(BF)
            out_ref[2 * pair + 1, at : at + ROWS, :] = jnp.where(low, swap_halves(a), b).astype(BF)
    group = lax.axis_index("zh") * 4 + lax.axis_index("x")
    docs = jnp.broadcast_to(doc_ref[...].astype(F32), (16, 640))
    docs = pltpu.roll(docs, lax.rem(640 - group * ROWS, 640), 1)[:, 0:128].astype(BF)
    for h in range(HEADS):
        out_ref[h, 2 * ROWS : 2 * ROWS + 16, :] = docs


def swap_edges(ref, off):
    first = ref[0:16, :]
    last = ref[LONG : LONG + 16, :]
    early = row_of(first) < off
    ref[0:16, :] = jnp.where(early, last, first)
    ref[LONG : LONG + 16, :] = jnp.where(early, first, last)


def columns_of(doc_row):
    return jnp.broadcast_to(doc_row, (128, doc_row.shape[1])).T


def order_kernel(in_ref, at_ref, qg_ref, kv_ref, doc_ref):
    doc_at = slice(2 * ROWS, 2 * ROWS + 16)
    long_doc = in_ref[8, doc_at, :].astype(F32)[0:1, 0:1]
    before = jnp.zeros((1, 128), F32)
    for b in range(16):
        row = in_ref[b, doc_at, :].astype(F32)[0:1, :]
        before += jnp.where((row < long_doc) & (lane_of(row) < ROWS), 1.0, 0.0)
        doc_ref[OWN * 2 + b * ROWS : OWN * 2 + (b + 1) * ROWS, :] = columns_of(row)[0:ROWS, :]
    start = jnp.sum(before).astype(jnp.int32)
    off = lax.rem(start, 16)
    at_ref[0] = start - off
    at_ref[1] = off
    first = lax.div(start, 16)

    def move(i, _):
        at = lax.rem(first + i, OWN // 16)
        chunk = lax.div(at, ROWS // 16)
        part = lax.rem(at, ROWS // 16) * 16
        rows = pl.ds(pl.multiple_of(i * 16, 16), 16)
        qg_ref[rows, :] = in_ref[chunk, pl.ds(pl.multiple_of(part, 16), 16), :]
        kv_ref[rows, :] = in_ref[chunk, pl.ds(pl.multiple_of(ROWS + part, 16), 16), :]
        doc_ref[rows, :] = doc_ref[pl.ds(pl.multiple_of(OWN * 2 + at * 16, 16), 16), :]
        return 0

    lax.fori_loop(0, OWN // 16, move, 0, unroll=8)
    for ref in (qg_ref, kv_ref, doc_ref):
        swap_edges(ref, off)
    docs = doc_ref[LONG : LONG + 384, :].T
    lines = [docs[0:1, n * 128 : n * 128 + 128] for n in range(3)]
    block = jnp.concatenate(lines + [jnp.zeros((13, 128), F32)], axis=0).astype(BF)
    qg_ref[OWN:SENT, :] = block
    kv_ref[OWN:SENT, :] = block


def doc_row_of(ref):
    lines = ref[OWN:SENT, :].astype(F32)
    return jnp.concatenate([lines[n : n + 1, :] for n in range(3)], axis=1)


def same_doc(doc_cols, doc_row):
    wide = jnp.concatenate([doc_cols] * 3, axis=1)
    return (wide == doc_row)[0:REST, 0:REST]


def halves(x):
    zero = jnp.zeros_like(x)
    low = lane_of(x) < HD
    return jnp.where(low, x, zero), jnp.where(low, zero, x)


def totals_tile(kv_refs, vet_ref, col_ref, qg_ref, block, stat_ref, stat_row):
    doc_row = doc_row_of(qg_ref.at[block])
    for q_at, q_width in ((0, LONG), (LONG, REST)):
        rest = q_at == LONG
        qg = qg_ref[block, q_at : q_at + q_width, :]
        q0, _ = halves(qg)
        starts = [(h, at) for h in range(2) for at in (range(LONG, OWN, REST) if rest else range(0, LONG, STEP))]
        scores, tops, outs = {}, [], []

        def finish(key):
            half, at = key
            s = scores.pop(key)
            mask = None
            if rest:
                mask = same_doc(col_ref[half], doc_row)
                s = jnp.where(mask, s, NEG)
            top = jnp.max(s, axis=0, keepdims=True) * LOG2_SCALE
            p = jnp.exp2(s * LOG2_SCALE - top)
            if rest:
                p = jnp.where(mask, p, 0.0)
            lane = half * WIDE + lane_at(at)
            outs.append(dot_nn(vet_ref[:, lane : lane + s.shape[0]], p.astype(BF)))
            tops.append(top)

        for n, (half, at) in enumerate(starts):
            width = REST if rest else STEP
            scores[half, at] = dot_nt(kv_refs[half][at : at + width, :], q0)
            if n:
                finish(starts[n - 1])
        finish(starts[-1])
        top = functools.reduce(jnp.maximum, tops)
        out = sum(o * jnp.exp2(t - top) for o, t in zip(outs, tops))
        total = out[0:1, :]
        grad_t = qg.astype(F32).T
        dot = jnp.sum(out[HD:, :] * grad_t[HD:, :], axis=0, keepdims=True)
        if rest:
            empty = total <= 0.0
            total = jnp.where(empty, 1.0, total)
            top = jnp.where(empty, NEG, top)
        lanes = slice(lane_at(q_at), lane_at(q_at) + q_width)
        stat_ref[stat_row, 0:1, lanes] = top + jnp.log2(total)
        stat_ref[stat_row, 1:2, lanes] = dot / total


def lane_at(row):
    return row // STEP * 256


def values_of(kvt_ref, vet_ref):
    kvt = kvt_ref[...]
    vet_ref[...] = jnp.where(row_of(kvt) < HD, jnp.ones_like(kvt), kvt)


def near_kernel(kv_ref, kv_far_ref, qg0, qg1, qg3, stat_ref, kvt_ref, vet_ref, col_ref, qg_ref):
    for half, ref in enumerate((kv_ref, kv_far_ref)):
        for at in (0, STEP, 2 * STEP, 3 * STEP, LONG):
            width = REST if at == LONG else STEP
            lanes = slice(half * WIDE + lane_at(at), half * WIDE + lane_at(at) + width)
            kvt_ref[:, lanes] = ref[at : at + width, :].astype(F32).T.astype(BF)
        col_ref[half] = columns_of(doc_row_of(ref))
    values_of(kvt_ref, vet_ref)
    for n, ref in enumerate((qg0, qg1, qg3)):
        qg_ref[n] = ref[...]

    def block(n, _):
        totals_tile((kv_ref, kv_far_ref), vet_ref, col_ref, qg_ref, n, stat_ref, n)
        return 0

    lax.fori_loop(0, 3, block, 0)


def far_kernel(kv_ref, kv_far_ref, kvt_ref, qg2, near_ref, stat_ref, vet_ref, col_ref, qg_ref, last_ref):
    for half, ref in enumerate((kv_ref, kv_far_ref)):
        col_ref[half] = columns_of(doc_row_of(ref))
    values_of(kvt_ref, vet_ref)
    qg_ref[0] = qg2[...]
    totals_tile((kv_ref, kv_far_ref), vet_ref, col_ref, qg_ref, 0, last_ref, 0)
    stat_ref[0:2, :] = near_ref[0]
    stat_ref[2:4, :] = near_ref[1]
    stat_ref[4:6, :] = last_ref[0]
    stat_ref[6:8, :] = near_ref[2]


def combined(stat_refs, block):
    lses = [ref[2 * ((block - k) % 4) : 2 * ((block - k) % 4) + 1, :] for k, ref in enumerate(stat_refs)]
    dots = [ref[2 * ((block - k) % 4) + 1 : 2 * ((block - k) % 4) + 2, :] for k, ref in enumerate(stat_refs)]
    top = functools.reduce(jnp.maximum, lses)
    shares = [jnp.exp2(one - top) for one in lses]
    whole = sum(shares)
    return top + jnp.log2(whole), sum(w * d for w, d in zip(shares, dots)) / whole


def pair_grads(block, half, qg_ref, kv_ref, kvt_ref, row_ref, col_ref, dq_ref, dkv_ref):
    doc_row = doc_row_of(qg_ref.at[block])
    doc_col = col_ref[half]
    for q_at, q_width in ((0, LONG), (LONG, REST)):
        rest = q_at == LONG
        q0, g0 = halves(qg_ref[block, q_at : q_at + q_width, :])
        lanes = slice(lane_at(q_at), lane_at(q_at) + q_width)
        lse, dot = row_ref[block, 0:1, lanes], row_ref[block, 1:2, lanes]
        acc = None
        for at in range(LONG, OWN, REST) if rest else range(0, LONG, STEP):
            width = REST if rest else STEP
            kv = kv_ref[half, at : at + width, :]
            p = jnp.exp2(dot_nt(kv, q0) * LOG2_SCALE - lse)
            if rest:
                p = jnp.where(same_doc(doc_col, doc_row), p, 0.0)
            ds = (p * (dot_nt(kv, g0) - dot)).astype(BF)
            dkv_ref[half, at : at + width, :] += dot_nn(p.astype(BF), g0) + dot_nn(ds, q0)
            part = dot_nn(kvt_ref[half, 0:HD, lane_at(at) : lane_at(at) + width], ds)
            acc = part if acc is None else acc + part
        acc = acc * SCALE
        dq_ref[block, q_at : q_at + q_width, :] += jnp.concatenate([acc, acc], axis=0).T


def first_grads_kernel(
    kv0, kv1, kvt_in, qg0, qg1, qg2, qg3, st0, st1, st2, st3,
    dq1_out, dq2_out, dq3_out, dkv_far_out, dq_own_out, dkv_own_out,
    qg_ref, kv_ref, kvt_ref, row_ref, col_ref, dq_ref, dkv_ref,
):
    for n, ref in enumerate((qg0, qg1, qg2, qg3)):
        qg_ref[n] = ref[...]
        row_ref[n, 0:1, :], row_ref[n, 1:2, :] = combined((st0, st1, st2, st3), n)
    for n, ref in enumerate((kv0, kv1)):
        kv_ref[n] = ref[...]
        kvt_ref[n] = kvt_in[0:HD, n * WIDE : (n + 1) * WIDE]
        col_ref[n] = columns_of(doc_row_of(ref))
    dq_ref[...] = jnp.zeros_like(dq_ref)
    dkv_ref[...] = jnp.zeros_like(dkv_ref)

    def pair(n, _):
        far = (n < 4).astype(jnp.int32)
        block = jnp.where(n < 4, n, n - 3)
        pair_grads(block, far, qg_ref, kv_ref, kvt_ref, row_ref, col_ref, dq_ref, dkv_ref)
        return 0

    lax.fori_loop(0, 7, pair, 0)
    low = lax.broadcasted_iota(jnp.int32, (OWN // 2, 128), 1) < HD
    for n, out in ((1, dq1_out), (2, dq2_out), (3, dq3_out)):
        out[...] = jnp.where(low, dq_ref[n, 0 : OWN // 2, :], dq_ref[n, OWN // 2 : OWN, :]).astype(BF)
    dkv_far_out[...] = dkv_ref[1].astype(BF)
    dq_own_out[0] = dq_ref[0]
    dkv_own_out[0] = dkv_ref[0]


def last_grads_kernel(
    kv0, kvt_in, qg0, st0, st1, st2, st3, dq_in, dkv_in, dq_out, dkv_out, qg_ref, kv_ref, kvt_ref, row_ref, col_ref
):
    qg_ref[0] = qg0[...]
    row_ref[0, 0:1, :], row_ref[0, 1:2, :] = combined((st0, st1, st2, st3), 0)
    kv_ref[0] = kv0[...]
    kvt_ref[0] = kvt_in[0:HD, 0:WIDE]
    col_ref[0] = columns_of(doc_row_of(kv0))
    dq_out[...] = dq_in[...]
    dkv_out[...] = dkv_in[...]
    pair_grads(0, 0, qg_ref, kv_ref, kvt_ref, row_ref, col_ref, dq_out, dkv_out)


def merge_kernel(at_ref, own_dq, dq1, dq2, dq3, own_dkv, far_dkv, out_ref, dq_ref, dkv_ref):
    half = OWN // 2
    far = dq1[...].astype(F32) + dq2[...].astype(F32) + dq3[...].astype(F32)
    turned = swap_halves(far)
    low = lane_of(far) < HD
    dq_ref[0:half, :] = own_dq[0, 0:half, :] + jnp.where(low, far, turned)
    dq_ref[half:OWN, :] = own_dq[0, half:OWN, :] + jnp.where(low, turned, far)
    dkv = own_dkv[0] + far_dkv[...].astype(F32)
    dkv_ref[...] = jnp.where(lane_of(dkv) < HD, dkv * SCALE, dkv)
    off = at_ref[1]
    swap_edges(dq_ref, off)
    swap_edges(dkv_ref, off)
    base = at_ref[0]

    def chunk(c, _):
        def sixteen(ref, n):
            spot = lax.rem(c * ROWS + 16 * n + OWN - base, OWN)
            return ref[pl.ds(pl.multiple_of(spot, 16), 16), :]

        for n in range(5):
            out_ref[c, 16 * n : 16 * n + 16, :] = sixteen(dkv_ref, n).astype(BF)
        groups = [sixteen(dq_ref, n) for n in range(5)]
        low = lane_of(groups[0]) < HD
        out_ref[c, 80:96, :] = jnp.where(low, groups[0], groups[1]).astype(BF)
        out_ref[c, 96:112, :] = jnp.where(low, groups[2], groups[3]).astype(BF)
        out_ref[c, 112:128, :] = groups[4].astype(BF)
        return 0

    lax.fori_loop(0, 16, chunk, 0)


def join_kernel(in_ref, q_out, k_out, v_out):
    for pair in range(HEADS // 2):
        cols = slice(pair * 128, pair * 128 + 128)
        a, b = in_ref[2 * pair].astype(F32), in_ref[2 * pair + 1].astype(F32)
        a_swap, b_swap = swap_halves(a), swap_halves(b)
        low = lane_of(a) < HD
        even, odd = jnp.where(low, a, b_swap).astype(BF), jnp.where(low, a_swap, b).astype(BF)
        k_out[:, cols] = even[0:ROWS]
        v_out[:, cols] = odd[0:ROWS]
        for n in range(5):
            part = slice(ROWS + 16 * (n // 2), ROWS + 16 * (n // 2) + 16)
            q_out[16 * n : 16 * n + 16, cols] = (odd if n % 2 else even)[part]


def shifted(array, by):
    return lax.ppermute(array, "x", [(i, (i + by) % 4) for i in range(4)])


def crossed(array):
    return lax.ppermute(array, "zh", [(0, 1), (1, 0)])


def body(queries, keys, values, out_grad, doc_ids):
    packed = call(
        pack_kernel,
        "pack",
        [shape(16, 176, 128)],
        [queries, keys, values, out_grad, doc_ids.reshape(1, 640)],
    )[0]
    packed = lax.all_to_all(packed, BLK, 0, 0, tiled=True)
    at, qg, kv = call(
        order_kernel,
        "order",
        [shape(2, dtype=jnp.int32), shape(SENT, 128), shape(SENT, 128)],
        [packed],
        smem_out=1,
        scratch=[pltpu.VMEM((3 * OWN, 128), F32)],
    )
    kv_far = crossed(kv)
    qgs = [qg, shifted(qg, 1), shifted(qg, 2), shifted(qg, 3)]

    vet = pltpu.VMEM((128, 2 * WIDE), BF)
    col = pltpu.VMEM((2, 384, 128), F32)
    near, kvt = call(
        near_kernel,
        "totals_near",
        [shape(3, 2, WIDE, dtype=F32), shape(128, 2 * WIDE)],
        [kv, kv_far, qgs[0], qgs[1], qgs[3]],
        scratch=[vet, col, pltpu.VMEM((3, SENT, 128), BF)],
        flops=7_500_000_000,
    )
    stats = call(
        far_kernel,
        "totals_far",
        [shape(8, WIDE, dtype=F32)],
        [kv, kv_far, kvt, qgs[2], near],
        scratch=[vet, col, pltpu.VMEM((1, SENT, 128), BF), pltpu.VMEM((1, 2, WIDE), F32)],
        flops=2_500_000_000,
    )[0]
    stats = [stats] + [shifted(stats, k) for k in (1, 2, 3)]

    dq1, dq2, dq3, dkv_far, dq_own, dkv_own = call(
        first_grads_kernel,
        "grads_far",
        [shape(OWN // 2, 128)] * 3
        + [shape(OWN, 128), shape(1, OWN, 128, dtype=F32), shape(1, OWN, 128, dtype=F32)],
        [kv, kv_far, kvt, *qgs, *stats],
        scratch=[
            pltpu.VMEM((4, SENT, 128), BF),
            pltpu.VMEM((2, SENT, 128), BF),
            pltpu.VMEM((2, HD, WIDE), BF),
            pltpu.VMEM((4, 2, WIDE), F32),
            col,
            pltpu.VMEM((4, OWN, 128), F32),
            pltpu.VMEM((2, OWN, 128), F32),
        ],
        flops=20_000_000_000,
    )
    dqs = [shifted(dq, -n) for n, dq in ((1, dq1), (2, dq2), (3, dq3))]
    dkv_far = crossed(dkv_far)
    dq_own, dkv_own = call(
        last_grads_kernel,
        "grads_own",
        [shape(1, OWN, 128, dtype=F32), shape(1, OWN, 128, dtype=F32)],
        [kv, kvt, qg, *stats, dq_own, dkv_own],
        scratch=[
            pltpu.VMEM((1, SENT, 128), BF),
            pltpu.VMEM((1, SENT, 128), BF),
            pltpu.VMEM((1, HD, WIDE), BF),
            pltpu.VMEM((1, 2, WIDE), F32),
            pltpu.VMEM((1, 384, 128), F32),
        ],
        flops=3_000_000_000,
    )
    merged = call(
        merge_kernel,
        "merge",
        [shape(16, 128, 128)],
        [at, dq_own, *dqs, dkv_own, dkv_far],
        smem_in=1,
        scratch=[pltpu.VMEM((OWN, 128), F32), pltpu.VMEM((OWN, 128), F32)],
    )[0]
    merged = lax.all_to_all(merged, BLK, 0, 0, tiled=True)
    return tuple(call(join_kernel, "join", [shape(ROWS, HEADS * HD)] * 3, [merged]))


def solution(mesh):
    fine = Mesh(mesh.devices.reshape(4, 2, 2, 2, 4), BLK + ("zh", "x"))
    rows = P(BLK + ("zh", "x"), None)
    return jax.shard_map(
        body,
        mesh=fine,
        in_specs=(rows, rows, rows, rows, P(BLK)),
        out_specs=(rows, rows, rows),
        check_vma=False,
    )
```

```python
import functools
import math

import jax
import jax.numpy as jnp
from jax import lax
from jax.experimental import pallas as pl
from jax.experimental.pallas import tpu as pltpu
from jax.sharding import Mesh
from jax.sharding import PartitionSpec as P

BF = jnp.bfloat16
F32 = jnp.float32
HD = 64
HEADS = 16
ROWS = 80
OWN = 1280
LONG = 960
REST = OWN - LONG
SENT = OWN + 16
CUT = 656
STEP = 240
WIDE = 1408
SCALE = 1.0 / math.sqrt(HD)
LOG2_SCALE = SCALE * math.log2(math.e)
NEG = -1e30
BLK = ("y", "zl", "c")
VMEM_LIMIT = 24 << 20


def dot_nt(a, b):
    return lax.dot_general(a, b, (((1,), (1,)), ((), ())), preferred_element_type=F32)


def dot_nn(a, b):
    return lax.dot_general(a, b, (((1,), (0,)), ((), ())), preferred_element_type=F32)


def lane_of(x):
    return lax.broadcasted_iota(jnp.int32, x.shape, x.ndim - 1)


def row_of(x):
    return lax.broadcasted_iota(jnp.int32, x.shape, 0)


def swap_halves(x):
    return pltpu.roll(x, HD, 1)


def shape(*dims, dtype=BF):
    return jax.ShapeDtypeStruct(dims, dtype)


def call(kernel, name, outs, args, smem_in=0, smem_out=0, scratch=(), flops=1 << 20, vmem=VMEM_LIMIT):
    vm = pl.BlockSpec(memory_space=pltpu.VMEM)
    sm = pl.BlockSpec(memory_space=pltpu.SMEM)
    return pl.pallas_call(
        kernel,
        out_shape=outs,
        in_specs=[sm] * smem_in + [vm] * (len(args) - smem_in),
        out_specs=[sm] * smem_out + [vm] * (len(outs) - smem_out),
        scratch_shapes=list(scratch),
        compiler_params=pltpu.CompilerParams(vmem_limit_bytes=vmem),
        cost_estimate=pl.CostEstimate(flops=flops, bytes_accessed=1 << 20, transcendentals=0),
        name=name,
    )(*args)


def pack_kernel(q_ref, k_ref, v_ref, g_ref, doc_ref, out_ref):
    for pair in range(HEADS // 2):
        cols = slice(pair * 128, pair * 128 + 128)
        for a_ref, b_ref, at in ((q_ref, g_ref, 0), (k_ref, v_ref, ROWS)):
            a = a_ref[:, cols].astype(F32)
            b = b_ref[:, cols].astype(F32)
            low = lane_of(a) < HD
            out_ref[2 * pair, at : at + ROWS, :] = jnp.where(low, a, swap_halves(b)).astype(BF)
            out_ref[2 * pair + 1, at : at + ROWS, :] = jnp.where(low, swap_halves(a), b).astype(BF)
    group = lax.axis_index("zh") * 4 + lax.axis_index("x")
    docs = jnp.broadcast_to(doc_ref[...].astype(F32), (16, 640))
    docs = pltpu.roll(docs, lax.rem(640 - group * ROWS, 640), 1)[:, 0:128].astype(BF)
    for h in range(HEADS):
        out_ref[h, 2 * ROWS : 2 * ROWS + 16, :] = docs


def swap_edges(ref, off):
    first = ref[0:16, :]
    last = ref[LONG : LONG + 16, :]
    early = row_of(first) < off
    ref[0:16, :] = jnp.where(early, last, first)
    ref[LONG : LONG + 16, :] = jnp.where(early, first, last)


def columns_of(doc_row):
    return jnp.broadcast_to(doc_row, (128, doc_row.shape[1])).T


def order_kernel(in_ref, at_ref, qg_ref, kv_ref, doc_ref):
    doc_at = slice(2 * ROWS, 2 * ROWS + 16)
    long_doc = in_ref[8, doc_at, :].astype(F32)[0:1, 0:1]
    before = jnp.zeros((1, 128), F32)
    for b in range(16):
        row = in_ref[b, doc_at, :].astype(F32)[0:1, :]
        before += jnp.where((row < long_doc) & (lane_of(row) < ROWS), 1.0, 0.0)
        doc_ref[OWN * 2 + b * ROWS : OWN * 2 + (b + 1) * ROWS, :] = columns_of(row)[0:ROWS, :]
    start = jnp.sum(before).astype(jnp.int32)
    off = lax.rem(start, 16)
    at_ref[0] = start - off
    at_ref[1] = off
    first = lax.div(start, 16)

    def move(i, _):
        at = lax.rem(first + i, OWN // 16)
        chunk = lax.div(at, ROWS // 16)
        part = lax.rem(at, ROWS // 16) * 16
        rows = pl.ds(pl.multiple_of(i * 16, 16), 16)
        qg_ref[rows, :] = in_ref[chunk, pl.ds(pl.multiple_of(part, 16), 16), :]
        kv_ref[rows, :] = in_ref[chunk, pl.ds(pl.multiple_of(ROWS + part, 16), 16), :]
        doc_ref[rows, :] = doc_ref[pl.ds(pl.multiple_of(OWN * 2 + at * 16, 16), 16), :]
        return 0

    lax.fori_loop(0, OWN // 16, move, 0, unroll=8)
    for ref in (qg_ref, kv_ref, doc_ref):
        swap_edges(ref, off)
    docs = doc_ref[LONG : LONG + 384, :].T
    lines = [docs[0:1, n * 128 : n * 128 + 128] for n in range(3)]
    block = jnp.concatenate(lines + [jnp.zeros((13, 128), F32)], axis=0).astype(BF)
    qg_ref[OWN:SENT, :] = block
    kv_ref[OWN:SENT, :] = block


def doc_row_of(ref):
    lines = ref[OWN:SENT, :].astype(F32)
    return jnp.concatenate([lines[n : n + 1, :] for n in range(3)], axis=1)


def same_doc(doc_cols, doc_row):
    wide = jnp.concatenate([doc_cols] * 3, axis=1)
    return (wide == doc_row)[0:REST, 0:REST]


def halves(x):
    zero = jnp.zeros_like(x)
    low = lane_of(x) < HD
    return jnp.where(low, x, zero), jnp.where(low, zero, x)


def totals_tile(kv_refs, vet_ref, col_ref, qg_ref, block, stat_ref):
    doc_row = doc_row_of(qg_ref.at[block])
    for q_at, q_width in ((0, LONG), (LONG, REST)):
        rest = q_at == LONG
        qg = qg_ref[block, q_at : q_at + q_width, :]
        q0, _ = halves(qg)
        steps = range(LONG, OWN, REST) if rest else range(0, LONG, STEP)
        starts = [(half, at) for half in range(len(kv_refs)) for at in steps]
        scores, tops, outs = {}, [], []

        def finish(key):
            half, at = key
            s = scores.pop(key)
            mask = None
            if rest:
                mask = same_doc(col_ref[half], doc_row)
                s = jnp.where(mask, s, NEG)
            top = jnp.max(s, axis=0, keepdims=True) * LOG2_SCALE
            p = jnp.exp2(s * LOG2_SCALE - top)
            if rest:
                p = jnp.where(mask, p, 0.0)
            lane = half * WIDE + lane_at(at)
            outs.append(dot_nn(vet_ref[:, lane : lane + s.shape[0]], p.astype(BF)))
            tops.append(top)

        for n, (half, at) in enumerate(starts):
            width = REST if rest else STEP
            scores[half, at] = dot_nt(kv_refs[half][at : at + width, :], q0)
            if n:
                finish(starts[n - 1])
        finish(starts[-1])
        top = functools.reduce(jnp.maximum, tops)
        out = sum(o * jnp.exp2(t - top) for o, t in zip(outs, tops))
        total = out[0:1, :]
        grad_t = qg.astype(F32).T
        dot = jnp.sum(out[HD:, :] * grad_t[HD:, :], axis=0, keepdims=True)
        if rest:
            empty = total <= 0.0
            total = jnp.where(empty, 1.0, total)
            top = jnp.where(empty, NEG, top)
        lanes = slice(lane_at(q_at), lane_at(q_at) + q_width)
        stat_ref[block, 0:1, lanes] = top + jnp.log2(total)
        stat_ref[block, 1:2, lanes] = dot / total


def lane_at(row):
    return row // STEP * 256


def prepare_keys(kv_refs, kvt_refs, vet_ref, col_ref, fresh):
    for half, (kv_ref, kvt_ref) in enumerate(zip(kv_refs, kvt_refs)):
        if fresh:
            for at in (0, STEP, 2 * STEP, 3 * STEP, LONG):
                width = REST if at == LONG else STEP
                kvt_ref[:, lane_at(at) : lane_at(at) + width] = (
                    kv_ref[at : at + width, :].astype(F32).T.astype(BF)
                )
        kvt = kvt_ref[...]
        vet_ref[:, half * WIDE : (half + 1) * WIDE] = jnp.where(
            row_of(kvt) < HD, jnp.ones_like(kvt), kvt
        )
        col_ref[half] = columns_of(doc_row_of(kv_ref))


def own_totals_kernel(kv_ref, qg_in, stat_ref, kvt_ref, vet_ref, col_ref, qg_ref):
    prepare_keys([kv_ref], [kvt_ref], vet_ref, col_ref, True)
    qg_ref[0] = qg_in[...]
    totals_tile([kv_ref], vet_ref, col_ref, qg_ref, 0, stat_ref)


def near_totals_kernel(kv0, kv1, kvt0, kvt1, qg1, qg3, stat_ref, vet_ref, col_ref, qg_ref):
    prepare_keys([kv0, kv1], [kvt0, kvt1], vet_ref, col_ref, False)
    qg_ref[0] = qg1[...]
    qg_ref[1] = qg3[...]

    def block(n, _):
        totals_tile([kv0, kv1], vet_ref, col_ref, qg_ref, n, stat_ref)
        return 0

    lax.fori_loop(0, 2, block, 0)


def added(pairs):
    top = functools.reduce(jnp.maximum, [lse for lse, _ in pairs])
    shares = [jnp.exp2(lse - top) for lse, _ in pairs]
    whole = sum(shares)
    return top + jnp.log2(whole), sum(w * dot for w, (_, dot) in zip(shares, pairs)) / whole


def far_totals_kernel(
    kv0, kv1, kvt0, kvt1, qg2a, qg2b, own_ref, own_far_ref, near_ref, stat_ref, qg_out,
    vet_ref, col_ref, qg_ref, last_ref,
):
    prepare_keys([kv0, kv1], [kvt0, kvt1], vet_ref, col_ref, False)
    qg_ref[0, 0:CUT, :] = qg2a[...]
    qg_ref[0, CUT:SENT, :] = qg2b[...]
    qg_out[...] = qg_ref[0]
    totals_tile([kv0, kv1], vet_ref, col_ref, qg_ref, 0, last_ref)
    lse, dot = added([(ref[0, 0:1, :], ref[0, 1:2, :]) for ref in (own_ref, own_far_ref)])
    stat_ref[0:1, :] = lse
    stat_ref[1:2, :] = dot
    stat_ref[2:4, :] = near_ref[0]
    stat_ref[4:6, :] = last_ref[0]
    stat_ref[6:8, :] = near_ref[1]


def combined(stat_refs, block):
    pairs = []
    for k, ref in enumerate(stat_refs):
        at = 2 * ((block - k) % 4)
        pairs.append((ref[at : at + 1, :], ref[at + 1 : at + 2, :]))
    return added(pairs)


def pair_grads(block, half, qg_ref, kv_ref, kvt_ref, row_ref, col_ref, dq_ref, dkv_ref):
    doc_row = doc_row_of(qg_ref.at[block])
    doc_col = col_ref[half]
    for q_at, q_width in ((0, LONG), (LONG, REST)):
        rest = q_at == LONG
        q0, g0 = halves(qg_ref[block, q_at : q_at + q_width, :])
        lanes = slice(lane_at(q_at), lane_at(q_at) + q_width)
        lse, dot = row_ref[block, 0:1, lanes], row_ref[block, 1:2, lanes]
        acc = None
        for at in range(LONG, OWN, REST) if rest else range(0, LONG, STEP):
            width = REST if rest else STEP
            kv = kv_ref[half, at : at + width, :]
            p = jnp.exp2(dot_nt(kv, q0) * LOG2_SCALE - lse)
            if rest:
                p = jnp.where(same_doc(doc_col, doc_row), p, 0.0)
            ds = (p * (dot_nt(kv, g0) - dot)).astype(BF)
            dkv_ref[half, at : at + width, :] += dot_nn(p.astype(BF), g0) + dot_nn(ds, q0)
            part = dot_nn(kvt_ref[half, 0:HD, lane_at(at) : lane_at(at) + width], ds)
            acc = part if acc is None else acc + part
        acc = acc * SCALE
        dq_ref[block, q_at : q_at + q_width, :] += jnp.concatenate([acc, acc], axis=0).T


def packed_dq(dq):
    low = lax.broadcasted_iota(jnp.int32, (OWN // 2, 128), 1) < HD
    return jnp.where(low, dq[0 : OWN // 2, :], dq[OWN // 2 : OWN, :])


def grads_kernel(plan, names, *refs):
    ref = dict(zip(names, refs))
    blocks, own_keys = plan["blocks"], plan["halves"]
    for n, block in enumerate(blocks):
        ref["qg_all"][n] = ref["qg", block][...]
        ref["row_all"][n] = ref["rows"][block]
        if ("dq_in", block) in ref:
            ref["dq_all"][n] = ref["dq_in", block][...]
        else:
            ref["dq_all"][n] = jnp.zeros((OWN, 128), F32)
    for n, half in enumerate(own_keys):
        ref["kv_all"][n] = ref["kv", half][...]
        ref["kvt_all"][n] = ref["kvt", half][0:HD, :]
        ref["col_all"][n] = columns_of(doc_row_of(ref["kv", half]))
        if ("dkv_in", half) in ref:
            ref["dkv_all"][n] = ref["dkv_in", half][...]
        else:
            ref["dkv_all"][n] = jnp.zeros((OWN, 128), F32)

    def pair(n, _):
        pair_grads(
            lax.div(n, len(own_keys)),
            lax.rem(n, len(own_keys)),
            *(ref[name] for name in ("qg_all", "kv_all", "kvt_all", "row_all", "col_all", "dq_all", "dkv_all")),
        )
        return 0

    lax.fori_loop(0, len(blocks) * len(own_keys), pair, 0)
    for n, block in enumerate(blocks):
        if ("dq_out", block) in ref:
            ref["dq_out", block][...] = ref["dq_all"][n]
    for n, half in enumerate(own_keys):
        if ("dkv_out", half) in ref:
            ref["dkv_out", half][...] = ref["dkv_all"][n]
        if ("dkv_send", half) in ref:
            ref["dkv_send", half][...] = ref["dkv_all"][n].astype(BF)
    if "dq_a" in ref:
        packed = packed_dq(ref["dq_all"][0]).astype(BF)
        ref["dq_a"][...] = packed[0 : OWN // 4, :]
        ref["dq_b"][...] = packed[OWN // 4 : OWN // 2, :]
    if "dq_send" in ref:
        packed = packed_dq(ref["dq_all"][0])
        relay = ref["relay"][...].astype(F32)
        first, second = packed[0 : OWN // 4, :], packed[OWN // 4 : OWN // 2, :]
        if blocks[0] == 3:
            first = first + relay
        else:
            second = second + relay
        ref["dq_send"][0 : OWN // 4, :] = first.astype(BF)
        ref["dq_send"][OWN // 4 : OWN // 2, :] = second.astype(BF)


def rows_kernel(st0, st1, st2, st3, row_ref):
    for n in range(4):
        row_ref[n, 0:1, :], row_ref[n, 1:2, :] = combined((st0, st1, st2, st3), n)


def grads(name, blocks, halves_, arrays, takes=(), gives=()):
    ins = [("kv", h) for h in halves_] + [("kvt", h) for h in halves_] + ["rows"]
    ins += [("qg", b) for b in blocks] + list(takes)
    shapes = {"dq_a": shape(OWN // 4, 128), "dq_b": shape(OWN // 4, 128), "dq_send": shape(OWN // 2, 128)}
    outs = [
        shapes[g] if g in shapes else shape(OWN, 128, dtype=BF if g[0] == "dkv_send" else F32)
        for g in gives
    ]
    nb, nh = len(blocks), len(halves_)
    scratch = dict(
        qg_all=pltpu.VMEM((nb, SENT, 128), BF),
        row_all=pltpu.VMEM((nb, 2, WIDE), F32),
        dq_all=pltpu.VMEM((nb, OWN, 128), F32),
        kv_all=pltpu.VMEM((nh, SENT, 128), BF),
        kvt_all=pltpu.VMEM((nh, HD, WIDE), BF),
        col_all=pltpu.VMEM((nh, 384, 128), F32),
        dkv_all=pltpu.VMEM((nh, OWN, 128), F32),
    )
    results = call(
        functools.partial(
            grads_kernel,
            dict(blocks=blocks, halves=halves_),
            ins + list(gives) + list(scratch),
        ),
        name,
        outs,
        [arrays[n] for n in ins],
        scratch=scratch.values(),
        flops=nb * nh * 3_000_000_000,
    )
    arrays.update(zip(gives, results))


def merge_kernel(at_ref, own_dq, dq1, dq3, own_dkv, far_dkv, out_ref, dq_ref, dkv_ref):
    half = OWN // 2
    far = dq1[...].astype(F32) + dq3[...].astype(F32)
    turned = swap_halves(far)
    low = lane_of(far) < HD
    dq_ref[0:half, :] = own_dq[0:half, :] + jnp.where(low, far, turned)
    dq_ref[half:OWN, :] = own_dq[half:OWN, :] + jnp.where(low, turned, far)
    dkv = own_dkv[...] + far_dkv[...].astype(F32)
    dkv_ref[...] = jnp.where(lane_of(dkv) < HD, dkv * SCALE, dkv)
    off = at_ref[1]
    swap_edges(dq_ref, off)
    swap_edges(dkv_ref, off)
    base = at_ref[0]

    def chunk(c, _):
        def sixteen(ref, n):
            spot = lax.rem(c * ROWS + 16 * n + OWN - base, OWN)
            return ref[pl.ds(pl.multiple_of(spot, 16), 16), :]

        for n in range(5):
            out_ref[c, 16 * n : 16 * n + 16, :] = sixteen(dkv_ref, n).astype(BF)
        groups = [sixteen(dq_ref, n) for n in range(5)]
        low = lane_of(groups[0]) < HD
        out_ref[c, 80:96, :] = jnp.where(low, groups[0], groups[1]).astype(BF)
        out_ref[c, 96:112, :] = jnp.where(low, groups[2], groups[3]).astype(BF)
        out_ref[c, 112:128, :] = groups[4].astype(BF)
        return 0

    lax.fori_loop(0, 16, chunk, 0)


def join_kernel(in_ref, q_out, k_out, v_out):
    for pair in range(HEADS // 2):
        cols = slice(pair * 128, pair * 128 + 128)
        a, b = in_ref[2 * pair].astype(F32), in_ref[2 * pair + 1].astype(F32)
        a_swap, b_swap = swap_halves(a), swap_halves(b)
        low = lane_of(a) < HD
        even, odd = jnp.where(low, a, b_swap).astype(BF), jnp.where(low, a_swap, b).astype(BF)
        k_out[:, cols] = even[0:ROWS]
        v_out[:, cols] = odd[0:ROWS]
        for n in range(5):
            part = slice(ROWS + 16 * (n // 2), ROWS + 16 * (n // 2) + 16)
            q_out[16 * n : 16 * n + 16, cols] = (odd if n % 2 else even)[part]


def shifted(array, by):
    return lax.ppermute(array, "x", [(i, (i + by) % 4) for i in range(4)])


def crossed(array):
    return lax.ppermute(array, "zh", [(0, 1), (1, 0)])


def body(queries, keys, values, out_grad, doc_ids):
    packed = call(
        pack_kernel,
        "pack",
        [shape(16, 176, 128)],
        [queries, keys, values, out_grad, doc_ids.reshape(1, 640)],
        vmem=56 << 20,
    )[0]
    packed = lax.all_to_all(packed, BLK, 0, 0, tiled=True)
    at, qg, kv = call(
        order_kernel,
        "order",
        [shape(2, dtype=jnp.int32), shape(SENT, 128), shape(SENT, 128)],
        [packed],
        smem_out=1,
        scratch=[pltpu.VMEM((3 * OWN, 128), F32)],
    )
    kv_far = crossed(kv)
    qg1, qg3 = shifted(qg, 1), shifted(qg, -1)
    qg2 = shifted(qg1[:CUT], 1), shifted(qg3[CUT:], -1)

    def side(sets, blocks):
        return [
            pltpu.VMEM((128, sets * WIDE), BF),
            pltpu.VMEM((sets, 384, 128), F32),
            pltpu.VMEM((blocks, SENT, 128), BF),
        ]

    own, kvt = call(
        own_totals_kernel,
        "totals_own",
        [shape(1, 2, WIDE, dtype=F32), shape(128, WIDE)],
        [kv, qg],
        scratch=side(1, 1),
        flops=1_250_000_000,
    )
    own_far, kvt_far = call(
        own_totals_kernel,
        "totals_own_far",
        [shape(1, 2, WIDE, dtype=F32), shape(128, WIDE)],
        [kv_far, qg],
        scratch=side(1, 1),
        flops=1_250_000_000,
    )
    near = call(
        near_totals_kernel,
        "totals_near",
        [shape(2, 2, WIDE, dtype=F32)],
        [kv, kv_far, kvt, kvt_far, qg1, qg3],
        scratch=side(2, 2),
        flops=5_000_000_000,
    )[0]
    stats, qg2 = call(
        far_totals_kernel,
        "totals_far",
        [shape(8, WIDE, dtype=F32), shape(SENT, 128)],
        [kv, kv_far, kvt, kvt_far, *qg2, own, own_far, near],
        scratch=side(2, 1) + [pltpu.VMEM((1, 2, WIDE), F32)],
        flops=2_500_000_000,
    )
    rows = call(
        rows_kernel,
        "rows",
        [shape(4, 2, WIDE, dtype=F32)],
        [stats] + [shifted(stats, k) for k in (1, 2, 3)],
    )[0]

    arrays = {("qg", n): one for n, one in enumerate((qg, qg1, qg2, qg3))}
    arrays.update({("kv", 0): kv, ("kv", 1): kv_far, ("kvt", 0): kvt, ("kvt", 1): kvt_far, "rows": rows})
    grads("grads_far", (2,), (0, 1), arrays, (), ("dq_a", "dq_b", ("dkv_out", 0), ("dkv_out", 1)))
    arrays["dkv_in", 0], arrays["dkv_in", 1] = arrays["dkv_out", 0], arrays["dkv_out", 1]
    to_three, to_one = shifted(arrays["dq_a"], 1), shifted(arrays["dq_b"], -1)
    three = ("dq_out", 1), ("dq_out", 3), ("dq_out", 0)
    grads("grads_partner", (1, 3, 0), (1,), arrays, [("dkv_in", 1)], [*three, ("dkv_send", 1)])
    for n in (0, 1, 3):
        arrays["dq_in", n] = arrays["dq_out", n]
    dkv_far = crossed(arrays["dkv_send", 1])
    sent = {}
    for n, relay, by in ((1, to_one, -1), (3, to_three, 1)):
        arrays["relay"] = relay
        takes = [("dkv_in", 0), ("dq_in", n), "relay"]
        grads(f"grads_near_{n}", (n,), (0,), arrays, takes, ["dq_send", ("dkv_out", 0)])
        arrays["dkv_in", 0] = arrays["dkv_out", 0]
        sent[n] = shifted(arrays["dq_send"], by)
    takes = [("dkv_in", 0), ("dq_in", 0)]
    grads("grads_own", (0,), (0,), arrays, takes, [("dq_out", 0), ("dkv_out", 0)])
    merged = call(
        merge_kernel,
        "merge",
        [shape(16, 128, 128)],
        [at, arrays["dq_out", 0], sent[1], sent[3], arrays["dkv_out", 0], dkv_far],
        smem_in=1,
        scratch=[pltpu.VMEM((OWN, 128), F32), pltpu.VMEM((OWN, 128), F32)],
    )[0]
    merged = lax.all_to_all(merged, BLK, 0, 0, tiled=True)
    return tuple(call(join_kernel, "join", [shape(ROWS, HEADS * HD)] * 3, [merged]))


def solution(mesh):
    fine = Mesh(mesh.devices.reshape(4, 2, 2, 2, 4), BLK + ("zh", "x"))
    rows = P(BLK + ("zh", "x"), None)
    return jax.shard_map(
        body,
        mesh=fine,
        in_specs=(rows, rows, rows, rows, P(BLK)),
        out_specs=(rows, rows, rows),
        check_vma=False,
    )
```

```python
import functools
import math

import jax
import jax.numpy as jnp
from jax import lax
from jax.experimental import pallas as pl
from jax.experimental.pallas import tpu as pltpu
from jax.sharding import Mesh
from jax.sharding import PartitionSpec as P

BF = jnp.bfloat16
F32 = jnp.float32
HD = 64
HEADS = 16
ROWS = 80
OWN = 1280
LONG = 960
REST = OWN - LONG
SENT = OWN + 16
CUT = 656
STEP = 240
WIDE = 1408
SCALE = 1.0 / math.sqrt(HD)
LOG2_SCALE = SCALE * math.log2(math.e)
NEG = -1e30
BLK = ("y", "zl", "c")
BY_HEAD = ("y", "zl", "zh")
VMEM_LIMIT = 24 << 20


def dot_nt(a, b):
    return lax.dot_general(a, b, (((1,), (1,)), ((), ())), preferred_element_type=F32)


def dot_nn(a, b):
    return lax.dot_general(a, b, (((1,), (0,)), ((), ())), preferred_element_type=F32)


def lane_of(x):
    return lax.broadcasted_iota(jnp.int32, x.shape, x.ndim - 1)


def row_of(x):
    return lax.broadcasted_iota(jnp.int32, x.shape, 0)


def swap_halves(x):
    return pltpu.roll(x, HD, 1)


def shape(*dims, dtype=BF):
    return jax.ShapeDtypeStruct(dims, dtype)


def call(kernel, name, outs, args, smem_in=0, smem_out=0, scratch=(), flops=1 << 20, vmem=VMEM_LIMIT):
    vm = pl.BlockSpec(memory_space=pltpu.VMEM)
    sm = pl.BlockSpec(memory_space=pltpu.SMEM)
    return pl.pallas_call(
        kernel,
        out_shape=outs,
        in_specs=[sm] * smem_in + [vm] * (len(args) - smem_in),
        out_specs=[sm] * smem_out + [vm] * (len(outs) - smem_out),
        scratch_shapes=list(scratch),
        compiler_params=pltpu.CompilerParams(vmem_limit_bytes=vmem),
        cost_estimate=pl.CostEstimate(flops=flops, bytes_accessed=1 << 20, transcendentals=0),
        name=name,
    )(*args)


def pack_kernel(q_ref, k_ref, v_ref, g_ref, doc_ref, out_ref):
    for pair in range(HEADS // 2):
        cols = slice(pair * 128, pair * 128 + 128)
        for a_ref, b_ref, at in ((q_ref, g_ref, 0), (k_ref, v_ref, ROWS)):
            a = a_ref[:, cols].astype(F32)
            b = b_ref[:, cols].astype(F32)
            low = lane_of(a) < HD
            out_ref[2 * pair, at : at + ROWS, :] = jnp.where(low, a, swap_halves(b)).astype(BF)
            out_ref[2 * pair + 1, at : at + ROWS, :] = jnp.where(low, swap_halves(a), b).astype(BF)
    group = lax.axis_index("zh") * 4 + lax.axis_index("x")
    docs = jnp.broadcast_to(doc_ref[...].astype(F32).reshape(1, 640), (16, 640))
    docs = pltpu.roll(docs, lax.rem(640 - group * ROWS, 640), 1)[:, 0:128].astype(BF)
    for h in range(HEADS):
        out_ref[h, 2 * ROWS : 2 * ROWS + 16, :] = docs


def swap_edges(ref, off):
    first = ref[0:16, :]
    last = ref[LONG : LONG + 16, :]
    early = row_of(first) < off
    ref[0:16, :] = jnp.where(early, last, first)
    ref[LONG : LONG + 16, :] = jnp.where(early, first, last)


def columns_of(doc_row):
    return jnp.broadcast_to(doc_row, (128, doc_row.shape[1])).T


def order_kernel(in_ref, at_ref, qg_ref, kv_ref, doc_ref):
    doc_at = slice(2 * ROWS, 2 * ROWS + 16)
    long_doc = in_ref[8, doc_at, :].astype(F32)[0:1, 0:1]
    before = jnp.zeros((1, 128), F32)
    for b in range(16):
        row = in_ref[b, doc_at, :].astype(F32)[0:1, :]
        before += jnp.where((row < long_doc) & (lane_of(row) < ROWS), 1.0, 0.0)
        doc_ref[OWN * 2 + b * ROWS : OWN * 2 + (b + 1) * ROWS, :] = columns_of(row)[0:ROWS, :]
    start = jnp.sum(before).astype(jnp.int32)
    off = lax.rem(start, 16)
    at_ref[0] = start - off
    at_ref[1] = off
    first = lax.div(start, 16)

    def move(i, _):
        at = lax.rem(first + i, OWN // 16)
        chunk = lax.div(at, ROWS // 16)
        part = lax.rem(at, ROWS // 16) * 16
        rows = pl.ds(pl.multiple_of(i * 16, 16), 16)
        qg_ref[rows, :] = in_ref[chunk, pl.ds(pl.multiple_of(part, 16), 16), :]
        kv_ref[rows, :] = in_ref[chunk, pl.ds(pl.multiple_of(ROWS + part, 16), 16), :]
        doc_ref[rows, :] = doc_ref[pl.ds(pl.multiple_of(OWN * 2 + at * 16, 16), 16), :]
        return 0

    lax.fori_loop(0, OWN // 16, move, 0, unroll=8)
    for ref in (qg_ref, kv_ref, doc_ref):
        swap_edges(ref, off)
    docs = doc_ref[LONG : LONG + 384, :].T
    lines = [docs[0:1, n * 128 : n * 128 + 128] for n in range(3)]
    block = jnp.concatenate(lines + [jnp.zeros((13, 128), F32)], axis=0).astype(BF)
    qg_ref[OWN:SENT, :] = block
    kv_ref[OWN:SENT, :] = block


def doc_row_of(ref):
    lines = ref[OWN:SENT, :].astype(F32)
    return jnp.concatenate([lines[n : n + 1, :] for n in range(3)], axis=1)


def same_doc(doc_cols, doc_row):
    wide = jnp.concatenate([doc_cols] * 3, axis=1)
    return (wide == doc_row)[0:REST, 0:REST]


def halves(x):
    zero = jnp.zeros_like(x)
    low = lane_of(x) < HD
    return jnp.where(low, x, zero), jnp.where(low, zero, x)


def totals_tile(kv_refs, vet_ref, col_ref, qg_ref, block, stat_ref, p_refs, top_refs):
    doc_row = doc_row_of(qg_ref.at[block])
    for q_at, q_width in ((0, LONG), (LONG, REST)):
        rest = q_at == LONG
        qg = qg_ref[block, q_at : q_at + q_width, :]
        q0, _ = halves(qg)
        steps = range(LONG, OWN, REST) if rest else range(0, LONG, STEP)
        starts = [(half, at) for half in range(len(kv_refs)) for at in steps]
        scores, tops, outs = {}, [], []

        def finish(key):
            half, at = key
            s = scores.pop(key)
            mask = None
            if rest:
                mask = same_doc(col_ref[half], doc_row)
                s = jnp.where(mask, s, NEG)
            top = jnp.max(s, axis=0, keepdims=True) * LOG2_SCALE
            p = jnp.exp2(s * LOG2_SCALE - top)
            if rest:
                p = jnp.where(mask, p, 0.0)
            lane = half * WIDE + lane_at(at)
            p = p.astype(BF)
            outs.append(dot_nn(vet_ref[:, lane : lane + s.shape[0]], p))
            tops.append(top)
            if not rest:
                p_refs[half][block, at : at + STEP, :] = p
                top_refs[half][block, at // STEP, :, 0:LONG] = top

        for n, (half, at) in enumerate(starts):
            width = REST if rest else STEP
            scores[half, at] = dot_nt(kv_refs[half][at : at + width, :], q0)
            if n:
                finish(starts[n - 1])
        finish(starts[-1])
        top = functools.reduce(jnp.maximum, tops)
        out = sum(o * jnp.exp2(t - top) for o, t in zip(outs, tops))
        total = out[0:1, :]
        grad_t = qg.astype(F32).T
        dot = jnp.sum(out[HD:, :] * grad_t[HD:, :], axis=0, keepdims=True)
        if rest:
            empty = total <= 0.0
            total = jnp.where(empty, 1.0, total)
            top = jnp.where(empty, NEG, top)
        lanes = slice(lane_at(q_at), lane_at(q_at) + q_width)
        stat_ref[block, 0:1, lanes] = top + jnp.log2(total)
        stat_ref[block, 1:2, lanes] = dot / total


def lane_at(row):
    return row // STEP * 256


def prepare_keys(kv_refs, kvt_refs, vet_ref, col_ref):
    for half, (kv_ref, kvt_ref) in enumerate(zip(kv_refs, kvt_refs)):
        for at in (0, STEP, 2 * STEP, 3 * STEP, LONG):
            width = REST if at == LONG else STEP
            kvt_ref[:, lane_at(at) : lane_at(at) + width] = (
                kv_ref[at : at + width, :].astype(F32).T.astype(BF)
            )
        kvt = kvt_ref[...]
        vet_ref[:, half * WIDE : (half + 1) * WIDE] = jnp.where(
            row_of(kvt) < HD, jnp.ones_like(kvt), kvt
        )
        col_ref[half] = columns_of(doc_row_of(kv_ref))


def totals_kernel(sets, *refs):
    kv_refs, refs = refs[:sets], refs[sets:]
    qg0, qg1, stat_ref = refs[:3]
    kvt_refs, p_refs, top_refs = (refs[3 + n * sets : 3 + (n + 1) * sets] for n in range(3))
    vet_ref, col_ref, qg_ref = refs[3 + 3 * sets :]
    prepare_keys(kv_refs, kvt_refs, vet_ref, col_ref)
    qg_ref[0] = qg0[...]
    qg_ref[1] = qg1[...]

    def block(n, _):
        totals_tile(kv_refs, vet_ref, col_ref, qg_ref, n, stat_ref, p_refs, top_refs)
        return 0

    lax.fori_loop(0, 2, block, 0)


def added(pairs):
    top = functools.reduce(jnp.maximum, [lse for lse, _ in pairs])
    shares = [jnp.exp2(lse - top) for lse, _ in pairs]
    whole = sum(shares)
    return top + jnp.log2(whole), sum(w * dot for w, (_, dot) in zip(shares, pairs)) / whole


def last_totals_kernel(
    kv2a, kv2b, qg0, qg1, first_ref, near_ref, stat_ref, kv_ref, kvt_ref, p_ref, top_ref,
    vet_ref, col_ref, qg_ref, last_ref,
):
    kv_ref[0:CUT, :] = kv2a[...]
    kv_ref[CUT:SENT, :] = kv2b[...]
    totals_kernel(1, kv_ref, qg0, qg1, last_ref, kvt_ref, p_ref, top_ref, vet_ref, col_ref, qg_ref)
    for n in range(2):
        parts = [(ref[n, 0:1, :], ref[n, 1:2, :]) for ref in (first_ref, near_ref, last_ref)]
        stat_ref[n, 0:1, :], stat_ref[n, 1:2, :] = added(parts)


def pair_grads(block, half, p_ref, top_ref, qg_ref, kv_ref, kvt_ref, row_ref, col_ref, dq_ref, dkv_ref):
    doc_row = doc_row_of(qg_ref.at[block])
    doc_col = col_ref[half]
    for q_at, q_width in ((0, LONG), (LONG, REST)):
        rest = q_at == LONG
        q0, g0 = halves(qg_ref[block, q_at : q_at + q_width, :])
        lanes = slice(lane_at(q_at), lane_at(q_at) + q_width)
        lse, dot = row_ref[block, 0:1, lanes], row_ref[block, 1:2, lanes]
        acc = None
        for at in range(LONG, OWN, REST) if rest else range(0, LONG, STEP):
            width = REST if rest else STEP
            kv = kv_ref[half, at : at + width, :]
            if rest:
                p = jnp.exp2(dot_nt(kv, q0) * LOG2_SCALE - lse)
                p = jnp.where(same_doc(doc_col, doc_row), p, 0.0)
            else:
                top = top_ref[block, at // STEP, :, 0:LONG]
                p = p_ref[block, at : at + STEP, :].astype(F32) * jnp.exp2(top - lse)
            ds = (p * (dot_nt(kv, g0) - dot)).astype(BF)
            dkv_ref[half, at : at + width, :] += dot_nn(p.astype(BF), g0) + dot_nn(ds, q0)
            part = dot_nn(kvt_ref[half, 0:HD, lane_at(at) : lane_at(at) + width], ds)
            acc = part if acc is None else acc + part
        acc = acc * SCALE
        dq_ref[block, q_at : q_at + q_width, :] += jnp.concatenate([acc, acc], axis=0).T


def packed_dq(dq):
    low = lax.broadcasted_iota(jnp.int32, (OWN // 2, 128), 1) < HD
    return jnp.where(low, dq[0 : OWN // 2, :], dq[OWN // 2 : OWN, :])


def grads_kernel(plan, names, *refs):
    ref = dict(zip(names, refs))
    blocks, own_keys = plan["blocks"], plan["halves"]
    for n, block in enumerate(blocks):
        ref["qg_all"][n] = ref["qg", block][...]
        if "rows" in ref:
            ref["row_all"][n] = ref["rows"][block]
        else:
            near, far = ref["stats"], ref["stats_far"]
            lse, dot = added([(r[k, 0:1, :], r[k, 1:2, :]) for r, k in ((near, n), (far, 1 - n))])
            ref["row_all"][n, 0:1, :] = lse
            ref["row_all"][n, 1:2, :] = dot
            ref["rows_out"][n] = ref["row_all"][n]
        if ("dq_in", block) in ref:
            ref["dq_all"][n] = ref["dq_in", block][...]
        else:
            ref["dq_all"][n] = jnp.zeros((OWN, 128), F32)
    for n, half in enumerate(own_keys):
        ref["kv_all"][n] = ref["kv", half][...]
        ref["kvt_all"][n] = ref["kvt", half][0:HD, :]
        ref["col_all"][n] = columns_of(doc_row_of(ref["kv", half]))
        if ("dkv_in", half) in ref:
            ref["dkv_all"][n] = ref["dkv_in", half][...]
        else:
            ref["dkv_all"][n] = jnp.zeros((OWN, 128), F32)

    def pair(n, _):
        pair_grads(
            lax.div(n, len(own_keys)),
            lax.rem(n, len(own_keys)),
            ref["p", own_keys[0]],
            ref["top", own_keys[0]],
            *(ref[name] for name in ("qg_all", "kv_all", "kvt_all", "row_all", "col_all", "dq_all", "dkv_all")),
        )
        return 0

    lax.fori_loop(0, len(blocks) * len(own_keys), pair, 0)
    for n, block in enumerate(blocks):
        if ("dq_out", block) in ref:
            ref["dq_out", block][...] = ref["dq_all"][n]
    for n, half in enumerate(own_keys):
        if ("dkv_out", half) in ref:
            ref["dkv_out", half][...] = ref["dkv_all"][n]
    if "dkv_send" in ref:
        ref["dkv_send"][...] = ref["dkv_all"][0].astype(BF)
    if "dq_send" in ref:
        ref["dq_send"][...] = packed_dq(ref["dq_all"][1]).astype(BF)


def grads(name, blocks, halves_, arrays, takes=(), gives=()):
    ins = [(kind, h) for kind in ("kv", "kvt", "p", "top") for h in halves_]
    ins += [("qg", b) for b in blocks] + list(takes)
    shapes = {
        "dkv_send": shape(OWN, 128),
        "dq_send": shape(OWN // 2, 128),
        "rows_out": shape(2, 2, WIDE, dtype=F32),
    }
    outs = [shapes[g] if g in shapes else shape(OWN, 128, dtype=F32) for g in gives]
    nb, nh = len(blocks), len(halves_)
    scratch = dict(
        qg_all=pltpu.VMEM((nb, SENT, 128), BF),
        row_all=pltpu.VMEM((nb, 2, WIDE), F32),
        dq_all=pltpu.VMEM((nb, OWN, 128), F32),
        kv_all=pltpu.VMEM((nh, SENT, 128), BF),
        kvt_all=pltpu.VMEM((nh, HD, WIDE), BF),
        col_all=pltpu.VMEM((nh, 384, 128), F32),
        dkv_all=pltpu.VMEM((nh, OWN, 128), F32),
    )
    results = call(
        functools.partial(
            grads_kernel,
            dict(blocks=blocks, halves=halves_),
            ins + list(gives) + list(scratch),
        ),
        name,
        outs,
        [arrays[n] for n in ins],
        scratch=scratch.values(),
        flops=nb * nh * 3_000_000_000,
    )
    arrays.update(zip(gives, results))


def merge_kernel(at_ref, own_dq, far_dq, own_dkv, dkv2, dkv1, dkv3, out_ref, dq_ref, dkv_ref):
    half = OWN // 2
    far = far_dq[...].astype(F32)
    turned = swap_halves(far)
    low = lane_of(far) < HD
    dq_ref[0:half, :] = own_dq[0:half, :] + jnp.where(low, far, turned)
    dq_ref[half:OWN, :] = own_dq[half:OWN, :] + jnp.where(low, turned, far)
    dkv = own_dkv[...] + sum(ref[...].astype(F32) for ref in (dkv2, dkv1, dkv3))
    dkv_ref[...] = jnp.where(lane_of(dkv) < HD, dkv * SCALE, dkv)
    off = at_ref[1]
    swap_edges(dq_ref, off)
    swap_edges(dkv_ref, off)
    base = at_ref[0]

    def chunk(c, _):
        def sixteen(ref, n):
            spot = lax.rem(c * ROWS + 16 * n + OWN - base, OWN)
            return ref[pl.ds(pl.multiple_of(spot, 16), 16), :]

        for n in range(5):
            out_ref[c, 16 * n : 16 * n + 16, :] = sixteen(dkv_ref, n).astype(BF)
        groups = [sixteen(dq_ref, n) for n in range(5)]
        low = lane_of(groups[0]) < HD
        out_ref[c, 80:96, :] = jnp.where(low, groups[0], groups[1]).astype(BF)
        out_ref[c, 96:112, :] = jnp.where(low, groups[2], groups[3]).astype(BF)
        out_ref[c, 112:128, :] = groups[4].astype(BF)
        return 0

    lax.fori_loop(0, 16, chunk, 0)


def join_kernel(in_ref, q_out, k_out, v_out):
    for pair in range(HEADS // 2):
        cols = slice(pair * 128, pair * 128 + 128)
        a, b = in_ref[2 * pair].astype(F32), in_ref[2 * pair + 1].astype(F32)
        a_swap, b_swap = swap_halves(a), swap_halves(b)
        low = lane_of(a) < HD
        even, odd = jnp.where(low, a, b_swap).astype(BF), jnp.where(low, a_swap, b).astype(BF)
        k_out[:, cols] = even[0:ROWS]
        v_out[:, cols] = odd[0:ROWS]
        for n in range(5):
            part = slice(ROWS + 16 * (n // 2), ROWS + 16 * (n // 2) + 16)
            q_out[16 * n : 16 * n + 16, cols] = (odd if n % 2 else even)[part]


def shifted(array, by):
    return lax.ppermute(array, "x", [(i, (i + by) % 4) for i in range(4)])


def crossed(array):
    return lax.ppermute(array, "c", [(0, 1), (1, 0)])


def body(queries, keys, values, out_grad, doc_ids):
    packed = call(
        pack_kernel,
        "pack",
        [shape(16, 176, 128)],
        [queries, keys, values, out_grad, doc_ids],
        vmem=56 << 20,
    )[0]
    packed = lax.all_to_all(packed, BY_HEAD, 0, 0, tiled=True)
    at, qg, kv = call(
        order_kernel,
        "order",
        [shape(2, dtype=jnp.int32), shape(SENT, 128), shape(SENT, 128)],
        [packed],
        smem_out=1,
        scratch=[pltpu.VMEM((3 * OWN, 128), F32)],
    )
    qg_far = crossed(qg)
    kv1, kv3 = shifted(kv, 1), shifted(kv, -1)

    def side(sets):
        return [
            pltpu.VMEM((128, sets * WIDE), BF),
            pltpu.VMEM((sets, 384, 128), F32),
            pltpu.VMEM((2, SENT, 128), BF),
        ]

    stat, turned = shape(2, 2, WIDE, dtype=F32), shape(128, WIDE)
    kept, kept_top = shape(2, LONG, LONG), shape(2, LONG // STEP, 1, 1024, dtype=F32)
    first, kvt0, p0, top0 = call(
        functools.partial(totals_kernel, 1),
        "totals_own",
        [stat, turned, kept, kept_top],
        [kv, qg, qg_far],
        scratch=side(1),
        flops=2_500_000_000,
    )
    kv1, kv3, first = lax.optimization_barrier((kv1, kv3, first))
    kv2 = shifted(kv1[:CUT], 1), shifted(kv3[CUT:], -1)
    near, kvt1, kvt3, p1, p3, top1, top3 = call(
        functools.partial(totals_kernel, 2),
        "totals_near",
        [stat, turned, turned, kept, kept, kept_top, kept_top],
        [kv1, kv3, qg, qg_far],
        scratch=side(2),
        flops=5_000_000_000,
    )
    stats, kv2, kvt2, p2, top2 = call(
        last_totals_kernel,
        "totals_far",
        [stat, shape(SENT, 128), turned, kept, kept_top],
        [*kv2, qg, qg_far, first, near],
        scratch=side(1) + [pltpu.VMEM((2, 2, WIDE), F32)],
        flops=2_500_000_000,
    )

    arrays = {("qg", 0): qg, ("qg", 1): qg_far, "stats": stats, "stats_far": crossed(stats)}
    arrays.update({("kv", n): one for n, one in enumerate((kv, kv1, kv2, kv3))})
    arrays.update({("kvt", n): one for n, one in enumerate((kvt0, kvt1, kvt2, kvt3))})
    arrays.update({("p", n): one for n, one in enumerate((p0, p1, p2, p3))})
    arrays.update({("top", n): one for n, one in enumerate((top0, top1, top2, top3))})
    both = (0, 1)
    dq_in, dq_out = [("dq_in", 0), ("dq_in", 1)], [("dq_out", 0), ("dq_out", 1)]

    def hand_on():
        for n in both:
            arrays["dq_in", n] = arrays["dq_out", n]

    takes, gives, sent = ["stats", "stats_far"], ["rows_out", *dq_out, "dkv_send"], []
    for name, n in (("grads_far", 2), ("grads_one", 1), ("grads_three", 3)):
        grads(name, both, (n,), arrays, takes, gives)
        hand_on()
        arrays["rows"] = arrays["rows_out"]
        takes, gives = ["rows", *dq_in], [*dq_out, "dkv_send"]
        sent.append(shifted(arrays["dkv_send"], -n))
    sent[0], arrays["dq_in", 0] = lax.optimization_barrier((sent[0], arrays["dq_in", 0]))
    grads("grads_own", both, (0,), arrays, ["rows", *dq_in], [("dq_out", 0), "dq_send", ("dkv_out", 0)])
    merged = call(
        merge_kernel,
        "merge",
        [shape(16, 128, 128)],
        [at, arrays["dq_out", 0], crossed(arrays["dq_send"]), arrays["dkv_out", 0], *sent],
        smem_in=1,
        scratch=[pltpu.VMEM((OWN, 128), F32), pltpu.VMEM((OWN, 128), F32)],
    )[0]
    merged = lax.all_to_all(merged, BY_HEAD, 0, 0, tiled=True)
    return tuple(call(join_kernel, "join", [shape(ROWS, HEADS * HD)] * 3, [merged]))


def solution(mesh):
    fine = Mesh(mesh.devices.reshape(4, 2, 2, 2, 4), BLK + ("zh", "x"))
    rows = P(BLK + ("zh", "x"), None)
    return jax.shard_map(
        body,
        mesh=fine,
        in_specs=(rows, rows, rows, rows, P(BLK)),
        out_specs=(rows, rows, rows),
        check_vma=False,
    )
```

```python
import functools
import math

import jax
import jax.numpy as jnp
from jax import lax
from jax.experimental import pallas as pl
from jax.experimental.pallas import tpu as pltpu
from jax.sharding import Mesh
from jax.sharding import PartitionSpec as P

BF = jnp.bfloat16
F32 = jnp.float32
HD = 64
HEADS = 16
ROWS = 80
OWN = 1280
LONG = 960
REST = OWN - LONG
SENT = OWN + 16
STEP = 240
WIDE = 1408
SCALE = 1.0 / math.sqrt(HD)
LOG2_SCALE = SCALE * math.log2(math.e)
NEG = -1e30
BLK = ("y", "zl", "c")
BY_HEAD = ("y", "zl", "zh")
VMEM_LIMIT = 24 << 20


def dot_nt(a, b):
    return lax.dot_general(a, b, (((1,), (1,)), ((), ())), preferred_element_type=F32)


def dot_nn(a, b):
    return lax.dot_general(a, b, (((1,), (0,)), ((), ())), preferred_element_type=F32)


def lane_of(x):
    return lax.broadcasted_iota(jnp.int32, x.shape, x.ndim - 1)


def row_of(x):
    return lax.broadcasted_iota(jnp.int32, x.shape, 0)


def swap_halves(x):
    return pltpu.roll(x, HD, 1)


def shape(*dims, dtype=BF):
    return jax.ShapeDtypeStruct(dims, dtype)


def call(kernel, name, outs, args, smem_in=0, smem_out=0, scratch=(), flops=1 << 20, vmem=VMEM_LIMIT):
    vm = pl.BlockSpec(memory_space=pltpu.VMEM)
    sm = pl.BlockSpec(memory_space=pltpu.SMEM)
    return pl.pallas_call(
        kernel,
        out_shape=outs,
        in_specs=[sm] * smem_in + [vm] * (len(args) - smem_in),
        out_specs=[sm] * smem_out + [vm] * (len(outs) - smem_out),
        scratch_shapes=list(scratch),
        compiler_params=pltpu.CompilerParams(vmem_limit_bytes=vmem),
        cost_estimate=pl.CostEstimate(flops=flops, bytes_accessed=1 << 20, transcendentals=0),
        name=name,
    )(*args)


def pack_kernel(q_ref, k_ref, v_ref, g_ref, doc_ref, out_ref):
    for pair in range(HEADS // 2):
        cols = slice(pair * 128, pair * 128 + 128)
        for a_ref, b_ref, at in ((q_ref, g_ref, 0), (k_ref, v_ref, ROWS)):
            a = a_ref[:, cols].astype(F32)
            b = b_ref[:, cols].astype(F32)
            low = lane_of(a) < HD
            out_ref[2 * pair, at : at + ROWS, :] = jnp.where(low, a, swap_halves(b)).astype(BF)
            out_ref[2 * pair + 1, at : at + ROWS, :] = jnp.where(low, swap_halves(a), b).astype(BF)
    group = lax.axis_index("zh") * 4 + lax.axis_index("x")
    docs = jnp.broadcast_to(doc_ref[...].astype(F32).reshape(1, 640), (16, 640))
    docs = pltpu.roll(docs, lax.rem(640 - group * ROWS, 640), 1)[:, 0:128].astype(BF)
    for h in range(HEADS):
        out_ref[h, 2 * ROWS : 2 * ROWS + 16, :] = docs


def swap_edges(ref, off):
    first = ref[0:16, :]
    last = ref[LONG : LONG + 16, :]
    early = row_of(first) < off
    ref[0:16, :] = jnp.where(early, last, first)
    ref[LONG : LONG + 16, :] = jnp.where(early, first, last)


def columns_of(doc_row):
    return jnp.broadcast_to(doc_row, (128, doc_row.shape[1])).T


def order_kernel(in_ref, at_ref, qg_ref, kv_ref, doc_ref):
    doc_at = slice(2 * ROWS, 2 * ROWS + 16)
    docs = jnp.concatenate([in_ref[b, doc_at, :].astype(F32)[0:1, :] for b in range(16)], axis=0)
    before = jnp.where((docs < docs[8:9, 0:1]) & (lane_of(docs) < ROWS), 1.0, 0.0)
    turned = jnp.concatenate([docs, jnp.zeros((112, 128), F32)], axis=0).T
    for b in range(16):
        doc_ref[OWN * 2 + b * ROWS : OWN * 2 + (b + 1) * ROWS, :] = jnp.broadcast_to(
            turned[0:ROWS, b : b + 1], (ROWS, 128)
        )
    start = jnp.sum(before).astype(jnp.int32)
    off = start & 15
    at_ref[0] = start - off
    at_ref[1] = off
    first = lax.shift_right_logical(start, 4)

    def place(i):
        at = first + i
        return at - jnp.where(at >= OWN // 16, OWN // 16, 0)

    def move(i, _):
        at = place(i)
        chunk = lax.shift_right_logical(at * 205, 10)
        part = (at - chunk * 5) * 16
        rows = pl.ds(pl.multiple_of(i * 16, 16), 16)
        qg_ref[rows, :] = in_ref[chunk, pl.ds(pl.multiple_of(part, 16), 16), :]
        kv_ref[rows, :] = in_ref[chunk, pl.ds(pl.multiple_of(ROWS + part, 16), 16), :]
        return 0

    lax.fori_loop(0, OWN // 16, move, 0, unroll=8)

    def move_docs(i, _):
        at = place(i) * 16
        rows = pl.ds(pl.multiple_of(i * 16, 16), 16)
        doc_ref[rows, :] = doc_ref[pl.ds(pl.multiple_of(OWN * 2 + at, 16), 16), :]
        return 0

    move_docs(0, 0)
    lax.fori_loop(LONG // 16, OWN // 16, move_docs, 0, unroll=4)
    for ref in (qg_ref, kv_ref, doc_ref):
        swap_edges(ref, off)
    docs = doc_ref[LONG : LONG + 384, :].T
    lines = [docs[0:1, n * 128 : n * 128 + 128] for n in range(3)]
    block = jnp.concatenate(lines + [jnp.zeros((13, 128), F32)], axis=0).astype(BF)
    qg_ref[OWN:SENT, :] = block
    kv_ref[OWN:SENT, :] = block


def doc_row_of(ref):
    lines = ref[OWN:SENT, :].astype(F32)
    return jnp.concatenate([lines[n : n + 1, :] for n in range(3)], axis=1)


def same_doc(doc_cols, doc_row):
    wide = jnp.concatenate([doc_cols] * (2 * REST // 128), axis=1)
    return (wide == doc_row)[0:REST, :]


def halves(x):
    zero = jnp.zeros_like(x)
    low = lane_of(x) < HD
    return jnp.where(low, x, zero), jnp.where(low, zero, x)


def totals_of(kv_refs, vet_ref, qg, grad_t, starts, mask_of, keep):
    q0, _ = halves(qg)
    scores, tops, outs = {}, [], []

    def finish(half, at, width):
        s = scores.pop((half, at))
        mask = mask_of(half) if mask_of else None
        if mask_of:
            s = jnp.where(mask, s, NEG)
        top = jnp.max(s, axis=0, keepdims=True) * LOG2_SCALE
        p = jnp.exp2(s * LOG2_SCALE - top)
        if mask_of:
            p = jnp.where(mask, p, 0.0)
        p = p.astype(BF)
        keep(half, at, p, top)
        lane = half * WIDE + lane_at(at)
        outs.append(dot_nn(vet_ref[:, lane : lane + width], p))
        tops.append(top)

    for n, (half, at, width) in enumerate(starts):
        scores[half, at] = dot_nt(kv_refs[half][at : at + width, :], q0)
        if n:
            finish(*starts[n - 1])
    finish(*starts[-1])
    top = functools.reduce(jnp.maximum, tops)
    shares = [jnp.exp2(t - top) for t in tops]
    total = sum(o[0:1, :] * w for o, w in zip(outs, shares))
    out = sum(o[HD:, :] * w for o, w in zip(outs, shares))
    dot = jnp.sum(out * grad_t.astype(F32), axis=0, keepdims=True)
    if mask_of:
        empty = total <= 0.0
        total = jnp.where(empty, 1.0, total)
        top = jnp.where(empty, NEG, top)
    return top + jnp.log2(total), dot / total


def lane_at(row):
    return row // STEP * 256


def prepare_keys(kv_refs, kvt_refs, vet_ref, col_ref):
    for half, (kv_ref, kvt_ref) in enumerate(zip(kv_refs, kvt_refs)):
        for at in (0, STEP, 2 * STEP, 3 * STEP, LONG):
            width = REST if at == LONG else STEP
            kvt_ref[:, lane_at(at) : lane_at(at) + width] = (
                kv_ref[at : at + width, :].T
            )
        kvt = kvt_ref[...]
        vet_ref[:, half * WIDE : (half + 1) * WIDE] = jnp.where(
            row_of(kvt) < HD, jnp.ones_like(kvt), kvt
        )
        col_ref[half] = columns_of(doc_row_of(kv_ref))


def rest_rows(first, second):
    return jnp.concatenate([first[LONG:OWN, :], second[LONG:OWN, :]], axis=0)


def totals(
    kv_refs, qg0, qg1, gt_ref, gt_rest_ref, stat_ref, kvt_refs, p_refs, rest_refs, top_refs,
    vet_ref, col_ref, qg_ref,
):
    prepare_keys(kv_refs, kvt_refs, vet_ref, col_ref)
    qg_ref[0] = qg0[0:LONG, :]
    qg_ref[1] = qg1[0:LONG, :]

    def block(n, _):
        def keep(half, at, p, top):
            p_refs[half][n, at : at + STEP, :] = p
            top_refs[half][n, at // STEP, :, 0:LONG] = top

        starts = [(half, at, STEP) for half in range(len(kv_refs)) for at in range(0, LONG, STEP)]
        lse, dot = totals_of(kv_refs, vet_ref, qg_ref[n], gt_ref[n], starts, None, keep)
        stat_ref[n, 0:1, 0:LONG] = lse
        stat_ref[n, 1:2, 0:LONG] = dot
        return 0

    lax.fori_loop(0, 2, block, 0)

    def keep_rest(half, at, p, top):
        rest_refs[half][...] = p
        top_refs[half][2, 0, :, 0 : 2 * REST] = top

    doc_row = jnp.concatenate([doc_row_of(ref)[:, 0:REST] for ref in (qg0, qg1)], axis=1)
    lse, dot = totals_of(
        kv_refs,
        vet_ref,
        rest_rows(qg0, qg1),
        gt_rest_ref[...],
        [(half, LONG, REST) for half in range(len(kv_refs))],
        lambda half: same_doc(col_ref[half], doc_row),
        keep_rest,
    )
    stat_ref[2, 0:1, 0 : 2 * REST] = lse
    stat_ref[2, 1:2, 0 : 2 * REST] = dot


def added(pairs):
    top = functools.reduce(jnp.maximum, [lse for lse, _ in pairs])
    shares = [jnp.exp2(lse - top) for lse, _ in pairs]
    whole = sum(shares)
    return top + jnp.log2(whole), sum(w * dot for w, (_, dot) in zip(shares, pairs)) / whole


def own_totals_kernel(
    kv, qg0, qg1, stat_ref, gt_ref, gt_rest_ref, kvt, p, rest, top, *scratch
):
    for n, ref in enumerate((qg0, qg1)):
        gt_ref[n] = ref[0:LONG, :].T[HD:, :]
    gt_rest_ref[...] = rest_rows(qg0, qg1).T[HD:, :]
    totals([kv], qg0, qg1, gt_ref, gt_rest_ref, stat_ref, [kvt], [p], [rest], [top], *scratch)


def near_totals_kernel(kv1, kv3, qg0, qg1, gt_ref, gt_rest_ref, stat_ref, *refs):
    kvts, ps, rests, tops = (refs[2 * n : 2 * n + 2] for n in range(4))
    totals(
        [kv1, kv3], qg0, qg1, gt_ref, gt_rest_ref, stat_ref, kvts, ps, rests, tops, *refs[8:]
    )


def last_totals_kernel(
    kv, qg0, qg1, gt_ref, gt_rest_ref, first_ref, near_ref,
    stat_ref, kvt, p, rest, top, vet_ref, col_ref, qg_ref, last_ref,
):
    totals(
        [kv], qg0, qg1, gt_ref, gt_rest_ref, last_ref, [kvt], [p], [rest], [top],
        vet_ref, col_ref, qg_ref,
    )
    for n in range(3):
        parts = [(ref[n, 0:1, :], ref[n, 1:2, :]) for ref in (first_ref, near_ref, last_ref)]
        stat_ref[n, 0:1, :], stat_ref[n, 1:2, :] = added(parts)


def tile_grads(qg, starts, weights_of, dot, kv_ref, kvt_ref, dkv_ref):
    q0, g0 = halves(qg)
    acc = None
    for at, width in starts:
        kv = kv_ref[at : at + width, :]
        p = weights_of(at)
        ds = (p * (dot_nt(kv, g0) - dot)).astype(BF)
        dkv_ref[at : at + width, :] += dot_nn(p.astype(BF), g0) + dot_nn(ds, q0)
        part = dot_nn(kvt_ref[0:HD, lane_at(at) : lane_at(at) + width], ds)
        acc = part if acc is None else acc + part
    return acc


def packed_dq(dq):
    low = lax.broadcasted_iota(jnp.int32, (OWN // 2, 128), 1) < HD
    return jnp.where(low, dq[0 : OWN // 2, :], dq[OWN // 2 : OWN, :])


def grads_kernel(names, *refs):
    ref = dict(zip(names, refs))
    dq_ref, dq_rest_ref, dkv_ref, row_ref = ref["dq"], ref["dq_rest"], ref["dkv"], ref["row"]
    kv_ref, kvt_ref, qg_ref = ref["kv"], ref["kvt"], ref["qg"]
    p_ref, rest_ref, top_ref = ref["p"], ref["rest"], ref["top"]
    if "rows" in ref:
        row_ref[...] = ref["rows"][...]
    else:
        for n in range(3):
            mine = [ref["stats"][n, k : k + 1, :] for k in range(2)]
            far = [ref["stats_far"][(1, 0, 2)[n], k : k + 1, :] for k in range(2)]
            if n == 2:
                far = [
                    jnp.concatenate([x[:, REST : 2 * REST], x[:, 0:REST], x[:, 2 * REST :]], axis=1)
                    for x in far
                ]
            row_ref[n, 0:1, :], row_ref[n, 1:2, :] = added([mine, far])
        ref["rows_out"][...] = row_ref[...]
    for n in range(2):
        qg_ref[n] = ref["qg", n][0:LONG, :]
    for out, known in ((dq_ref, "dq_in"), (dq_rest_ref, "dq_rest_in")):
        out[...] = ref[known][...] if known in ref else jnp.zeros_like(out)
    dkv_ref[...] = jnp.zeros_like(dkv_ref)

    def block(n, _):
        lse = row_ref[n, 0:1, 0:LONG]

        def weights_of(at):
            share = jnp.exp2(top_ref[n, at // STEP, :, 0:LONG] - lse)
            return p_ref[n, at : at + STEP, :].astype(F32) * share

        starts = [(at, STEP) for at in range(0, LONG, STEP)]
        dot = row_ref[n, 1:2, 0:LONG]
        dq_ref[n] += tile_grads(qg_ref[n], starts, weights_of, dot, kv_ref, kvt_ref, dkv_ref)
        return 0

    lax.fori_loop(0, 2, block, 0)
    both = slice(0, 2 * REST)
    share = jnp.exp2(top_ref[2, 0, :, both] - row_ref[2, 0:1, both])
    dq_rest_ref[...] += tile_grads(
        rest_rows(ref["qg", 0], ref["qg", 1]),
        [(LONG, REST)],
        lambda at: rest_ref[...].astype(F32) * share,
        row_ref[2, 1:2, both],
        kv_ref,
        kvt_ref,
        dkv_ref,
    )
    if "dkv_out" in ref:
        ref["dkv_out"][...] = dkv_ref[...]
    if "dkv_send" in ref:
        relay = ref["relay"][...].astype(F32) if "relay" in ref else 0.0
        ref["dkv_send"][...] = (dkv_ref[...] + relay).astype(BF)
    if "dq_send" in ref:
        rows_ref = ref["dq_rows"]
        rest = jnp.concatenate([dq_rest_ref[...] * SCALE] * 2, axis=0).T
        for n, out in enumerate((ref["dq_out"], rows_ref)):
            out[0:LONG, :] = jnp.concatenate([dq_ref[n] * SCALE] * 2, axis=0).T
            out[LONG:OWN, :] = rest[n * REST : (n + 1) * REST, :]
        ref["dq_send"][...] = packed_dq(rows_ref[...]).astype(BF)


def grads(name, keys, arrays, takes, gives, flops=6_000_000_000):
    arrays.update(keys)
    ins = [*keys, ("qg", 0), ("qg", 1), *takes]
    shapes = {
        "dq": shape(2, HD, LONG, dtype=F32),
        "dq_rest": shape(HD, 2 * REST, dtype=F32),
        "dkv_send": shape(OWN, 128),
        "dq_send": shape(OWN // 2, 128),
        "rows_out": shape(3, 2, 1024, dtype=F32),
    }
    scratch = dict(
        dkv=pltpu.VMEM((OWN, 128), F32),
        row=pltpu.VMEM((3, 2, 1024), F32),
        qg=pltpu.VMEM((2, LONG, 128), BF),
    )
    if "dq_send" in gives:
        scratch["dq"] = pltpu.VMEM((2, HD, LONG), F32)
        scratch["dq_rest"] = pltpu.VMEM((HD, 2 * REST), F32)
        scratch["dq_rows"] = pltpu.VMEM((OWN, 128), F32)
    results = call(
        functools.partial(grads_kernel, ins + list(gives) + list(scratch)),
        name,
        [shapes[g] if g in shapes else shape(OWN, 128, dtype=F32) for g in gives],
        [arrays[n] for n in ins],
        scratch=scratch.values(),
        flops=flops,
    )
    arrays.update(zip(gives, results))


def merge_kernel(at_ref, own_dq, far_dq, own_dkv, dkv1, dkv3, out_ref, dq_ref, dkv_ref):
    half = OWN // 2
    far = far_dq[...].astype(F32)
    turned = swap_halves(far)
    low = lane_of(far) < HD
    dq_ref[0:half, :] = own_dq[0:half, :] + jnp.where(low, far, turned)
    dq_ref[half:OWN, :] = own_dq[half:OWN, :] + jnp.where(low, turned, far)
    dkv = own_dkv[...] + sum(ref[...].astype(F32) for ref in (dkv1, dkv3))
    dkv_ref[...] = jnp.where(lane_of(dkv) < HD, dkv * SCALE, dkv)
    off = at_ref[1]
    swap_edges(dq_ref, off)
    swap_edges(dkv_ref, off)
    base = at_ref[0]

    def chunk(c, _):
        def sixteen(ref, n):
            spot = c * ROWS + 16 * n - base
            spot = spot + jnp.where(spot < 0, OWN, 0)
            return ref[pl.ds(pl.multiple_of(spot, 16), 16), :]

        for n in range(5):
            out_ref[c, 16 * n : 16 * n + 16, :] = sixteen(dkv_ref, n).astype(BF)
        groups = [sixteen(dq_ref, n) for n in range(5)]
        low = lane_of(groups[0]) < HD
        out_ref[c, 80:96, :] = jnp.where(low, groups[0], groups[1]).astype(BF)
        out_ref[c, 96:112, :] = jnp.where(low, groups[2], groups[3]).astype(BF)
        out_ref[c, 112:128, :] = groups[4].astype(BF)
        return 0

    lax.fori_loop(0, 16, chunk, 0)


def join_kernel(in_ref, q_out, k_out, v_out):
    for pair in range(HEADS // 2):
        cols = slice(pair * 128, pair * 128 + 128)
        a, b = in_ref[2 * pair].astype(F32), in_ref[2 * pair + 1].astype(F32)
        a_swap, b_swap = swap_halves(a), swap_halves(b)
        low = lane_of(a) < HD
        even, odd = jnp.where(low, a, b_swap).astype(BF), jnp.where(low, a_swap, b).astype(BF)
        k_out[:, cols] = even[0:ROWS]
        v_out[:, cols] = odd[0:ROWS]
        for n in range(5):
            part = slice(ROWS + 16 * (n // 2), ROWS + 16 * (n // 2) + 16)
            q_out[16 * n : 16 * n + 16, cols] = (odd if n % 2 else even)[part]


def shifted(array, by):
    pairs = [
        (c * 4 + x, c * 4 + (x + (by if c == 0 else -by)) % 4) for c in range(2) for x in range(4)
    ]
    return lax.ppermute(array, ("c", "x"), pairs)


def crossed(array):
    return lax.ppermute(array, "c", [(0, 1), (1, 0)])


def body(queries, keys, values, out_grad, doc_ids):
    packed = call(
        pack_kernel,
        "pack",
        [shape(16, 176, 128)],
        [queries, keys, values, out_grad, doc_ids],
        vmem=56 << 20,
    )[0]
    packed = lax.all_to_all(packed, BY_HEAD, 0, 0, tiled=True)
    at, qg, kv = call(
        order_kernel,
        "order",
        [shape(2, dtype=jnp.int32), shape(SENT, 128), shape(SENT, 128)],
        [packed],
        smem_out=1,
        scratch=[pltpu.VMEM((3 * OWN, 128), F32)],
    )
    qg_far = crossed(qg)
    kv1, kv3 = shifted(kv, 1), shifted(kv, -1)

    def side(sets):
        return [
            pltpu.VMEM((128, sets * WIDE), BF),
            pltpu.VMEM((sets, 384, 128), F32),
            pltpu.VMEM((2, LONG, 128), BF),
        ]

    stat, turned = shape(3, 2, 1024, dtype=F32), shape(128, WIDE)
    kept, kept_rest = shape(2, LONG, LONG), shape(REST, 2 * REST)
    kept_top = shape(3, LONG // STEP, 1, 1024, dtype=F32)
    grad_t = [shape(2, HD, LONG), shape(HD, 2 * REST)]
    first, *grad_t, kvt0, p0, rest0, top0 = call(
        own_totals_kernel,
        "totals_own",
        [stat, *grad_t, turned, kept, kept_rest, kept_top],
        [kv, qg, qg_far],
        scratch=side(1),
        flops=2_500_000_000,
    )
    kv1, kv3, first = lax.optimization_barrier((kv1, kv3, first))
    kv2 = shifted(kv1, 1)
    near, kvt1, kvt3, p1, p3, rest1, rest3, top1, top3 = call(
        near_totals_kernel,
        "totals_near",
        [stat] + [turned] * 2 + [kept] * 2 + [kept_rest] * 2 + [kept_top] * 2,
        [kv1, kv3, qg, qg_far, *grad_t],
        scratch=side(2),
        flops=5_000_000_000,
    )
    stats, kvt2, p2, rest2, top2 = call(
        last_totals_kernel,
        "totals_far",
        [stat, turned, kept, kept_rest, kept_top],
        [kv2, qg, qg_far, *grad_t, first, near],
        scratch=side(1) + [pltpu.VMEM((3, 2, 1024), F32)],
        flops=2_500_000_000,
    )

    sets = [
        dict(zip(("kv", "kvt", "p", "rest", "top"), one))
        for one in (
            (kv, kvt0, p0, rest0, top0),
            (kv1, kvt1, p1, rest1, top1),
            (kv2, kvt2, p2, rest2, top2),
            (kv3, kvt3, p3, rest3, top3),
        )
    ]
    arrays = {("qg", 0): qg, ("qg", 1): qg_far, "stats": stats, "stats_far": crossed(stats)}
    takes, gives = ["stats", "stats_far"], ["rows_out", "dq", "dq_rest", "dkv_send"]
    sent = {}
    for name, n, by in (("grads_far", 2, 1), ("grads_one", 1, -1), ("grads_three", 3, 1)):
        grads(name, sets[n], arrays, takes, gives)
        arrays["rows"] = arrays["rows_out"]
        arrays["dq_in"], arrays["dq_rest_in"] = arrays["dq"], arrays["dq_rest"]
        takes, gives = ["rows", "dq_in", "dq_rest_in"], ["dq", "dq_rest", "dkv_send"]
        sent[n] = shifted(arrays["dkv_send"], by)
        if n == 1:
            arrays["relay"] = sent[2]
            takes = [*takes, "relay"]
    sent[1], arrays["dq_in"] = lax.optimization_barrier((sent[1], arrays["dq_in"]))
    grads("grads_own", sets[0], arrays, takes, ["dq_out", "dq_send", "dkv_out"])
    merged = call(
        merge_kernel,
        "merge",
        [shape(16, 128, 128)],
        [at, arrays["dq_out"], crossed(arrays["dq_send"]), arrays["dkv_out"], sent[1], sent[3]],
        smem_in=1,
        scratch=[pltpu.VMEM((OWN, 128), F32), pltpu.VMEM((OWN, 128), F32)],
    )[0]
    merged = lax.all_to_all(merged, BY_HEAD, 0, 0, tiled=True)
    return tuple(call(join_kernel, "join", [shape(ROWS, HEADS * HD)] * 3, [merged]))


def solution(mesh):
    fine = Mesh(mesh.devices.reshape(4, 2, 2, 2, 4), BLK + ("zh", "x"))
    rows = P(BLK + ("zh", "x"), None)
    return jax.shard_map(
        body,
        mesh=fine,
        in_specs=(rows, rows, rows, rows, P(BLK)),
        out_specs=(rows, rows, rows),
        check_vma=False,
    )
```

```python
import functools
import math

import jax
import jax.numpy as jnp
from jax import lax
from jax.experimental import pallas as pl
from jax.experimental.pallas import tpu as pltpu
from jax.sharding import Mesh
from jax.sharding import PartitionSpec as P

BF = jnp.bfloat16
F32 = jnp.float32
HD = 64
HEADS = 16
ROWS = 80
OWN = 1280
LONG = 960
REST = OWN - LONG
SENT = OWN + 16
STEP = 240
WIDE = 1408
SCALE = 1.0 / math.sqrt(HD)
LOG2_SCALE = SCALE * math.log2(math.e)
NEG = -1e30
BLK = ("y", "zl", "c")
BY_HEAD = ("y", "zl", "zh")
VMEM_LIMIT = 24 << 20


def dot_nt(a, b):
    return lax.dot_general(a, b, (((1,), (1,)), ((), ())), preferred_element_type=F32)


def dot_nn(a, b):
    return lax.dot_general(a, b, (((1,), (0,)), ((), ())), preferred_element_type=F32)


def lane_of(x):
    return lax.broadcasted_iota(jnp.int32, x.shape, x.ndim - 1)


def row_of(x):
    return lax.broadcasted_iota(jnp.int32, x.shape, 0)


def swap_halves(x):
    return pltpu.roll(x, HD, 1)


def shape(*dims, dtype=BF):
    return jax.ShapeDtypeStruct(dims, dtype)


def call(kernel, name, outs, args, smem_in=0, smem_out=0, scratch=(), flops=1 << 20, vmem=VMEM_LIMIT):
    vm = pl.BlockSpec(memory_space=pltpu.VMEM)
    sm = pl.BlockSpec(memory_space=pltpu.SMEM)
    return pl.pallas_call(
        kernel,
        out_shape=outs,
        in_specs=[sm] * smem_in + [vm] * (len(args) - smem_in),
        out_specs=[sm] * smem_out + [vm] * (len(outs) - smem_out),
        scratch_shapes=list(scratch),
        compiler_params=pltpu.CompilerParams(vmem_limit_bytes=vmem),
        cost_estimate=pl.CostEstimate(flops=flops, bytes_accessed=1 << 20, transcendentals=0),
        name=name,
    )(*args)


def pack_kernel(q_ref, k_ref, v_ref, g_ref, doc_ref, out_ref):
    for pair in range(HEADS // 2):
        cols = slice(pair * 128, pair * 128 + 128)
        for a_ref, b_ref, at in ((q_ref, g_ref, 0), (k_ref, v_ref, ROWS)):
            a = a_ref[:, cols].astype(F32)
            b = b_ref[:, cols].astype(F32)
            low = lane_of(a) < HD
            out_ref[2 * pair, at : at + ROWS, :] = jnp.where(low, a, swap_halves(b)).astype(BF)
            out_ref[2 * pair + 1, at : at + ROWS, :] = jnp.where(low, swap_halves(a), b).astype(BF)
    group = lax.axis_index("zh") * 4 + lax.axis_index("x")
    docs = jnp.broadcast_to(doc_ref[...].astype(F32).reshape(1, 640), (16, 640))
    docs = pltpu.roll(docs, lax.rem(640 - group * ROWS, 640), 1)[:, 0:128].astype(BF)
    for h in range(HEADS):
        out_ref[h, 2 * ROWS : 2 * ROWS + 16, :] = docs


def swap_edges(ref, off):
    first = ref[0:16, :]
    last = ref[LONG : LONG + 16, :]
    early = row_of(first) < off
    ref[0:16, :] = jnp.where(early, last, first)
    ref[LONG : LONG + 16, :] = jnp.where(early, first, last)


def columns_of(doc_row):
    return jnp.broadcast_to(doc_row, (128, doc_row.shape[1])).T


def order_kernel(in_ref, at_ref, qg_ref, kv_ref, doc_ref):
    doc_at = slice(2 * ROWS, 2 * ROWS + 16)
    docs = jnp.concatenate([in_ref[b, doc_at, :].astype(F32)[0:1, :] for b in range(16)], axis=0)
    before = jnp.where((docs < docs[8:9, 0:1]) & (lane_of(docs) < ROWS), 1.0, 0.0)
    turned = jnp.concatenate([docs, jnp.zeros((112, 128), F32)], axis=0).T
    for b in range(16):
        doc_ref[OWN * 2 + b * ROWS : OWN * 2 + (b + 1) * ROWS, :] = jnp.broadcast_to(
            turned[0:ROWS, b : b + 1], (ROWS, 128)
        )
    start = jnp.sum(before).astype(jnp.int32)
    off = start & 15
    at_ref[0] = start - off
    at_ref[1] = off
    first = lax.shift_right_logical(start, 4)

    def place(i):
        at = first + i
        return at - jnp.where(at >= OWN // 16, OWN // 16, 0)

    def move(i, _):
        at = place(i)
        chunk = lax.shift_right_logical(at * 205, 10)
        part = (at - chunk * 5) * 16
        rows = pl.ds(pl.multiple_of(i * 16, 16), 16)
        qg_ref[rows, :] = in_ref[chunk, pl.ds(pl.multiple_of(part, 16), 16), :]
        kv_ref[rows, :] = in_ref[chunk, pl.ds(pl.multiple_of(ROWS + part, 16), 16), :]
        return 0

    lax.fori_loop(0, OWN // 16, move, 0, unroll=8)

    def move_docs(i, _):
        at = place(i) * 16
        rows = pl.ds(pl.multiple_of(i * 16, 16), 16)
        doc_ref[rows, :] = doc_ref[pl.ds(pl.multiple_of(OWN * 2 + at, 16), 16), :]
        return 0

    move_docs(0, 0)
    lax.fori_loop(LONG // 16, OWN // 16, move_docs, 0, unroll=4)
    for ref in (qg_ref, kv_ref, doc_ref):
        swap_edges(ref, off)
    docs = doc_ref[LONG : LONG + 384, :].T
    lines = [docs[0:1, n * 128 : n * 128 + 128] for n in range(3)]
    block = jnp.concatenate(lines + [jnp.zeros((13, 128), F32)], axis=0).astype(BF)
    qg_ref[OWN:SENT, :] = block
    kv_ref[OWN:SENT, :] = block


def doc_row_of(ref):
    lines = ref[OWN:SENT, :].astype(F32)
    return jnp.concatenate([lines[n : n + 1, :] for n in range(3)], axis=1)


def same_doc(doc_cols, doc_row):
    wide = jnp.concatenate([doc_cols] * (2 * REST // 128), axis=1)
    return (wide == doc_row)[0:REST, :]


def halves(x):
    zero = jnp.zeros_like(x)
    low = lane_of(x) < HD
    return jnp.where(low, x, zero), jnp.where(low, zero, x)


def totals_of(kv_refs, vet_ref, qg, grad_t, starts, mask_of, keep):
    q0, _ = halves(qg)
    scores, tops, outs = {}, [], []

    def finish(half, at, width):
        s = scores.pop((half, at))
        mask = mask_of(half) if mask_of else None
        if mask_of:
            s = jnp.where(mask, s, NEG)
        top = jnp.max(s, axis=0, keepdims=True) * LOG2_SCALE
        p = jnp.exp2(s * LOG2_SCALE - top)
        if mask_of:
            p = jnp.where(mask, p, 0.0)
        p = p.astype(BF)
        keep(half, at, p, top)
        lane = half * WIDE + lane_at(at)
        outs.append(dot_nn(vet_ref[:, lane : lane + width], p))
        tops.append(top)

    for n, (half, at, width) in enumerate(starts):
        scores[half, at] = dot_nt(kv_refs[half][at : at + width, :], q0)
        if n:
            finish(*starts[n - 1])
    finish(*starts[-1])
    top = functools.reduce(jnp.maximum, tops)
    shares = [jnp.exp2(t - top) for t in tops]
    total = sum(o[0:1, :] * w for o, w in zip(outs, shares))
    out = sum(o[HD:, :] * w for o, w in zip(outs, shares))
    dot = jnp.sum(out * grad_t.astype(F32), axis=0, keepdims=True)
    if mask_of:
        empty = total <= 0.0
        total = jnp.where(empty, 1.0, total)
        top = jnp.where(empty, NEG, top)
    return top + jnp.log2(total), dot / total


def lane_at(row):
    return row // STEP * 256


def prepare_keys(kv_refs, kvt_refs, vet_ref, col_ref):
    for half, (kv_ref, kvt_ref) in enumerate(zip(kv_refs, kvt_refs)):
        for at in (0, STEP, 2 * STEP, 3 * STEP, LONG):
            width = REST if at == LONG else STEP
            kvt_ref[:, lane_at(at) : lane_at(at) + width] = (
                kv_ref[at : at + width, :].T
            )
        kvt = kvt_ref[...]
        vet_ref[:, half * WIDE : (half + 1) * WIDE] = jnp.where(
            row_of(kvt) < HD, jnp.ones_like(kvt), kvt
        )
        col_ref[half] = columns_of(doc_row_of(kv_ref))


def rest_rows(first, second):
    return jnp.concatenate([first[LONG:OWN, :], second[LONG:OWN, :]], axis=0)


def totals(
    kv_refs, qg0, qg1, gt_ref, gt_rest_ref, stat_ref, kvt_refs, p_refs, rest_refs, top_refs,
    vet_ref, col_ref, qg_ref,
):
    prepare_keys(kv_refs, kvt_refs, vet_ref, col_ref)
    qg_ref[0] = qg0[0:LONG, :]
    qg_ref[1] = qg1[0:LONG, :]

    def block(n, _):
        def keep(half, at, p, top):
            p_refs[half][n, at : at + STEP, :] = p
            top_refs[half][n, at // STEP, :, 0:LONG] = top

        starts = [(half, at, STEP) for half in range(len(kv_refs)) for at in range(0, LONG, STEP)]
        lse, dot = totals_of(kv_refs, vet_ref, qg_ref[n], gt_ref[n], starts, None, keep)
        stat_ref[n, 0:1, 0:LONG] = lse
        stat_ref[n, 1:2, 0:LONG] = dot
        return 0

    for n in range(2):
        block(n, 0)

    def keep_rest(half, at, p, top):
        rest_refs[half][...] = p
        top_refs[half][2, 0, :, 0 : 2 * REST] = top

    doc_row = jnp.concatenate([doc_row_of(ref)[:, 0:REST] for ref in (qg0, qg1)], axis=1)
    lse, dot = totals_of(
        kv_refs,
        vet_ref,
        rest_rows(qg0, qg1),
        gt_rest_ref[...],
        [(half, LONG, REST) for half in range(len(kv_refs))],
        lambda half: same_doc(col_ref[half], doc_row),
        keep_rest,
    )
    stat_ref[2, 0:1, 0 : 2 * REST] = lse
    stat_ref[2, 1:2, 0 : 2 * REST] = dot


def added(pairs):
    top = functools.reduce(jnp.maximum, [lse for lse, _ in pairs])
    shares = [jnp.exp2(lse - top) for lse, _ in pairs]
    whole = sum(shares)
    return top + jnp.log2(whole), sum(w * dot for w, (_, dot) in zip(shares, pairs)) / whole


def own_totals_kernel(
    kv, qg0, qg1, stat_ref, gt_ref, gt_rest_ref, kvt, p, rest, top, *scratch
):
    for n, ref in enumerate((qg0, qg1)):
        gt_ref[n] = ref[0:LONG, :].T[HD:, :]
    gt_rest_ref[...] = rest_rows(qg0, qg1).T[HD:, :]
    totals([kv], qg0, qg1, gt_ref, gt_rest_ref, stat_ref, [kvt], [p], [rest], [top], *scratch)


def near_totals_kernel(kv1, kv3, qg0, qg1, gt_ref, gt_rest_ref, stat_ref, *refs):
    kvts, ps, rests, tops = (refs[2 * n : 2 * n + 2] for n in range(4))
    totals(
        [kv1, kv3], qg0, qg1, gt_ref, gt_rest_ref, stat_ref, kvts, ps, rests, tops, *refs[8:]
    )


def last_totals_kernel(
    kv, qg0, qg1, gt_ref, gt_rest_ref, first_ref, near_ref,
    stat_ref, kvt, p, rest, top, vet_ref, col_ref, qg_ref, last_ref,
):
    totals(
        [kv], qg0, qg1, gt_ref, gt_rest_ref, last_ref, [kvt], [p], [rest], [top],
        vet_ref, col_ref, qg_ref,
    )
    for n in range(3):
        parts = [(ref[n, 0:1, :], ref[n, 1:2, :]) for ref in (first_ref, near_ref, last_ref)]
        stat_ref[n, 0:1, :], stat_ref[n, 1:2, :] = added(parts)


def tile_grads(qg, starts, weights_of, dot, kv_ref, kvt_ref, dkv_ref):
    q0, g0 = halves(qg)
    acc = None
    for at, width in starts:
        kv = kv_ref[at : at + width, :]
        p = weights_of(at)
        ds = (p * (dot_nt(kv, g0) - dot)).astype(BF)
        dkv_ref[at : at + width, :] += dot_nn(p.astype(BF), g0) + dot_nn(ds, q0)
        part = dot_nn(kvt_ref[0:HD, lane_at(at) : lane_at(at) + width], ds)
        acc = part if acc is None else acc + part
    return acc


def packed_dq(dq):
    low = lax.broadcasted_iota(jnp.int32, (OWN // 2, 128), 1) < HD
    return jnp.where(low, dq[0 : OWN // 2, :], dq[OWN // 2 : OWN, :])


def grads_kernel(blocks, with_rest, names, *refs):
    ref = dict(zip(names, refs))
    dq_ref, dq_rest_ref, dkv_ref, row_ref = ref["dq"], ref["dq_rest"], ref["dkv"], ref["row"]
    kv_ref, kvt_ref, qg_ref = ref["kv"], ref["kvt"], ref["qg"]
    p_ref, rest_ref, top_ref = ref["p"], ref["rest"], ref["top"]
    if "rows" in ref:
        row_ref[...] = ref["rows"][...]
    else:
        for n in range(3):
            mine = [ref["stats"][n, k : k + 1, :] for k in range(2)]
            far = [ref["stats_far"][(1, 0, 2)[n], k : k + 1, :] for k in range(2)]
            if n == 2:
                far = [
                    jnp.concatenate([x[:, REST : 2 * REST], x[:, 0:REST], x[:, 2 * REST :]], axis=1)
                    for x in far
                ]
            row_ref[n, 0:1, :], row_ref[n, 1:2, :] = added([mine, far])
        ref["rows_out"][...] = row_ref[...]
    for n in range(2):
        qg_ref[n] = ref["qg", n][0:LONG, :]
    for out, known in ((dq_ref, "dq_in"), (dq_rest_ref, "dq_rest_in")):
        out[...] = ref[known][...] if known in ref else jnp.zeros_like(out)
    dkv_ref[...] = ref["dkv_in"][...] if "dkv_in" in ref else jnp.zeros_like(dkv_ref)

    def block(n, _):
        lse = row_ref[n, 0:1, 0:LONG]

        def weights_of(at):
            share = jnp.exp2(top_ref[n, at // STEP, :, 0:LONG] - lse)
            return p_ref[n, at : at + STEP, :].astype(F32) * share

        starts = [(at, STEP) for at in range(0, LONG, STEP)]
        dot = row_ref[n, 1:2, 0:LONG]
        dq_ref[n] += tile_grads(qg_ref[n], starts, weights_of, dot, kv_ref, kvt_ref, dkv_ref)
        return 0

    for n in blocks:
        block(n, 0)
    if with_rest:
        both = slice(0, 2 * REST)
        share = jnp.exp2(top_ref[2, 0, :, both] - row_ref[2, 0:1, both])
        dq_rest_ref[...] += tile_grads(
            rest_rows(ref["qg", 0], ref["qg", 1]),
            [(LONG, REST)],
            lambda at: rest_ref[...].astype(F32) * share,
            row_ref[2, 1:2, both],
            kv_ref,
            kvt_ref,
            dkv_ref,
        )
    if "dkv_out" in ref:
        ref["dkv_out"][...] = dkv_ref[...]
    if "dkv_send" in ref:
        relay = ref["relay"][...].astype(F32) if "relay" in ref else 0.0
        ref["dkv_send"][...] = (dkv_ref[...] + relay).astype(BF)
    for n, (whole, name) in enumerate((("dq_out", "dq_out"), ("dq_send", "dq_rows"))):
        if whole in ref:
            rest = dq_rest_ref[:, n * REST : (n + 1) * REST] * SCALE
            ref[name][0:LONG, :] = jnp.concatenate([dq_ref[n] * SCALE] * 2, axis=0).T
            ref[name][LONG:OWN, :] = jnp.concatenate([rest] * 2, axis=0).T
    if "dq_send" in ref:
        ref["dq_send"][...] = packed_dq(ref["dq_rows"][...]).astype(BF)


def grads(name, keys, arrays, takes, gives, blocks=(0, 1), with_rest=True):
    arrays.update(keys)
    ins = [*keys, ("qg", 0), ("qg", 1), *takes]
    shapes = {
        "dq": shape(2, HD, LONG, dtype=F32),
        "dq_rest": shape(HD, 2 * REST, dtype=F32),
        "dkv_send": shape(OWN, 128),
        "dq_send": shape(OWN // 2, 128),
        "rows_out": shape(3, 2, 1024, dtype=F32),
    }
    scratch = dict(
        dkv=pltpu.VMEM((OWN, 128), F32),
        row=pltpu.VMEM((3, 2, 1024), F32),
        qg=pltpu.VMEM((2, LONG, 128), BF),
    )
    if "dq" not in gives:
        scratch["dq"] = pltpu.VMEM((2, HD, LONG), F32)
    if "dq_rest" not in gives:
        scratch["dq_rest"] = pltpu.VMEM((HD, 2 * REST), F32)
    if "dq_send" in gives:
        scratch["dq_rows"] = pltpu.VMEM((OWN, 128), F32)
    results = call(
        functools.partial(grads_kernel, blocks, with_rest, ins + list(gives) + list(scratch)),
        name,
        [shapes[g] if g in shapes else shape(OWN, 128, dtype=F32) for g in gives],
        [arrays[n] for n in ins],
        scratch=scratch.values(),
        flops=3_000_000_000 * len(blocks),
    )
    arrays.update(zip(gives, results))


def merge_kernel(at_ref, own_dq, far_dq, own_dkv, dkv1, dkv3, out_ref, dq_ref, dkv_ref):
    half = OWN // 2
    far = far_dq[...].astype(F32)
    turned = swap_halves(far)
    low = lane_of(far) < HD
    dq_ref[0:half, :] = own_dq[0:half, :] + jnp.where(low, far, turned)
    dq_ref[half:OWN, :] = own_dq[half:OWN, :] + jnp.where(low, turned, far)
    dkv = own_dkv[...] + sum(ref[...].astype(F32) for ref in (dkv1, dkv3))
    dkv_ref[...] = jnp.where(lane_of(dkv) < HD, dkv * SCALE, dkv)
    off = at_ref[1]
    swap_edges(dq_ref, off)
    swap_edges(dkv_ref, off)
    base = at_ref[0]

    def chunk(c, _):
        def sixteen(ref, n):
            spot = c * ROWS + 16 * n - base
            spot = spot + jnp.where(spot < 0, OWN, 0)
            return ref[pl.ds(pl.multiple_of(spot, 16), 16), :]

        for n in range(5):
            out_ref[c, 16 * n : 16 * n + 16, :] = sixteen(dkv_ref, n).astype(BF)
        groups = [sixteen(dq_ref, n) for n in range(5)]
        low = lane_of(groups[0]) < HD
        out_ref[c, 80:96, :] = jnp.where(low, groups[0], groups[1]).astype(BF)
        out_ref[c, 96:112, :] = jnp.where(low, groups[2], groups[3]).astype(BF)
        out_ref[c, 112:128, :] = groups[4].astype(BF)
        return 0

    lax.fori_loop(0, 16, chunk, 0)


def join_kernel(in_ref, q_out, k_out, v_out):
    for pair in range(HEADS // 2):
        cols = slice(pair * 128, pair * 128 + 128)
        a, b = in_ref[2 * pair].astype(F32), in_ref[2 * pair + 1].astype(F32)
        a_swap, b_swap = swap_halves(a), swap_halves(b)
        low = lane_of(a) < HD
        even, odd = jnp.where(low, a, b_swap).astype(BF), jnp.where(low, a_swap, b).astype(BF)
        k_out[:, cols] = even[0:ROWS]
        v_out[:, cols] = odd[0:ROWS]
        for n in range(5):
            part = slice(ROWS + 16 * (n // 2), ROWS + 16 * (n // 2) + 16)
            q_out[16 * n : 16 * n + 16, cols] = (odd if n % 2 else even)[part]


def shifted(array, by):
    pairs = [
        (c * 4 + x, c * 4 + (x + (by if c == 0 else -by)) % 4) for c in range(2) for x in range(4)
    ]
    return lax.ppermute(array, ("c", "x"), pairs)


def crossed(array):
    return lax.ppermute(array, "c", [(0, 1), (1, 0)])


def body(queries, keys, values, out_grad, doc_ids):
    packed = call(
        pack_kernel,
        "pack",
        [shape(16, 176, 128)],
        [queries, keys, values, out_grad, doc_ids],
        vmem=56 << 20,
    )[0]
    packed = lax.all_to_all(packed, BY_HEAD, 0, 0, tiled=True)
    at, qg, kv = call(
        order_kernel,
        "order",
        [shape(2, dtype=jnp.int32), shape(SENT, 128), shape(SENT, 128)],
        [packed],
        smem_out=1,
        scratch=[pltpu.VMEM((3 * OWN, 128), F32)],
    )
    qg_far = crossed(qg)
    kv1, kv3 = shifted(kv, 1), shifted(kv, -1)

    def side(sets):
        return [
            pltpu.VMEM((128, sets * WIDE), BF),
            pltpu.VMEM((sets, 384, 128), F32),
            pltpu.VMEM((2, LONG, 128), BF),
        ]

    stat, turned = shape(3, 2, 1024, dtype=F32), shape(128, WIDE)
    kept, kept_rest = shape(2, LONG, LONG), shape(REST, 2 * REST)
    kept_top = shape(3, LONG // STEP, 1, 1024, dtype=F32)
    grad_t = [shape(2, HD, LONG), shape(HD, 2 * REST)]
    first, *grad_t, kvt0, p0, rest0, top0 = call(
        own_totals_kernel,
        "totals_own",
        [stat, *grad_t, turned, kept, kept_rest, kept_top],
        [kv, qg, qg_far],
        scratch=side(1),
        flops=2_500_000_000,
    )
    kv1, kv3, first = lax.optimization_barrier((kv1, kv3, first))
    kv2 = shifted(kv1, 1)
    near, kvt1, kvt3, p1, p3, rest1, rest3, top1, top3 = call(
        near_totals_kernel,
        "totals_near",
        [stat] + [turned] * 2 + [kept] * 2 + [kept_rest] * 2 + [kept_top] * 2,
        [kv1, kv3, qg, qg_far, *grad_t],
        scratch=side(2),
        flops=5_000_000_000,
    )
    stats, kvt2, p2, rest2, top2 = call(
        last_totals_kernel,
        "totals_far",
        [stat, turned, kept, kept_rest, kept_top],
        [kv2, qg, qg_far, *grad_t, first, near],
        scratch=side(1) + [pltpu.VMEM((3, 2, 1024), F32)],
        flops=2_500_000_000,
    )

    sets = [
        dict(zip(("kv", "kvt", "p", "rest", "top"), one))
        for one in (
            (kv, kvt0, p0, rest0, top0),
            (kv1, kvt1, p1, rest1, top1),
            (kv2, kvt2, p2, rest2, top2),
            (kv3, kvt3, p3, rest3, top3),
        )
    ]
    arrays = {("qg", 0): qg, ("qg", 1): qg_far, "stats": stats, "stats_far": crossed(stats)}
    takes, gives = ["stats", "stats_far"], ["rows_out", "dq", "dq_rest", "dkv_send"]
    sent = {}
    for name, n, by in (("grads_far", 2, 1), ("grads_one", 1, -1), ("grads_three", 3, 1)):
        grads(name, sets[n], arrays, takes, gives)
        arrays["rows"] = arrays["rows_out"]
        arrays["dq_in"], arrays["dq_rest_in"] = arrays["dq"], arrays["dq_rest"]
        takes, gives = ["rows", "dq_in", "dq_rest_in"], ["dq", "dq_rest", "dkv_send"]
        sent[n] = shifted(arrays["dkv_send"], by)
        if n == 1:
            arrays["relay"] = sent[2]
            takes = [*takes, "relay"]
    takes = ["rows", "dq_in", "dq_rest_in"]
    gives = ["dq_send", "dq_rest", "dkv_out"]
    grads("grads_own_far", sets[0], arrays, takes, gives, blocks=(1,))
    far_dq = crossed(arrays["dq_send"])
    arrays["dkv_in"], arrays["dq_rest_in"] = arrays["dkv_out"], arrays["dq_rest"]
    sent[1], arrays["dq_in"] = lax.optimization_barrier((sent[1], arrays["dq_in"]))
    grads(
        "grads_own", sets[0], arrays, [*takes, "dkv_in"], ["dq_out", "dkv_out"], (0,), False
    )
    merged = call(
        merge_kernel,
        "merge",
        [shape(16, 128, 128)],
        [at, arrays["dq_out"], far_dq, arrays["dkv_out"], sent[1], sent[3]],
        smem_in=1,
        scratch=[pltpu.VMEM((OWN, 128), F32), pltpu.VMEM((OWN, 128), F32)],
    )[0]
    merged = lax.all_to_all(merged, BY_HEAD, 0, 0, tiled=True)
    return tuple(call(join_kernel, "join", [shape(ROWS, HEADS * HD)] * 3, [merged]))


def solution(mesh):
    fine = Mesh(mesh.devices.reshape(4, 2, 2, 2, 4), BLK + ("zh", "x"))
    rows = P(BLK + ("zh", "x"), None)
    return jax.shard_map(
        body,
        mesh=fine,
        in_specs=(rows, rows, rows, rows, P(BLK)),
        out_specs=(rows, rows, rows),
        check_vma=False,
    )
```

```python
import functools
import math

import jax
import jax.numpy as jnp
from jax import lax
from jax.experimental import pallas as pl
from jax.experimental.pallas import tpu as pltpu
from jax.sharding import Mesh
from jax.sharding import PartitionSpec as P

BF = jnp.bfloat16
F32 = jnp.float32
HD = 64
HEADS = 16
ROWS = 80
OWN = 1280
LONG = 960
REST = OWN - LONG
SENT = OWN + 16
STEP = 240
WIDE = 1408
SCALE = 1.0 / math.sqrt(HD)
LOG2_SCALE = SCALE * math.log2(math.e)
NEG = -1e30
BLK = ("y", "zl", "c")
BY_HEAD = ("y", "zl", "zh")
VMEM_LIMIT = 24 << 20


def dot_nt(a, b):
    return lax.dot_general(a, b, (((1,), (1,)), ((), ())), preferred_element_type=F32)


def dot_nn(a, b):
    return lax.dot_general(a, b, (((1,), (0,)), ((), ())), preferred_element_type=F32)


def lane_of(x):
    return lax.broadcasted_iota(jnp.int32, x.shape, x.ndim - 1)


def row_of(x):
    return lax.broadcasted_iota(jnp.int32, x.shape, 0)


def swap_halves(x):
    return pltpu.roll(x, HD, 1)


def shape(*dims, dtype=BF):
    return jax.ShapeDtypeStruct(dims, dtype)


def call(kernel, name, outs, args, smem_in=0, smem_out=0, scratch=(), flops=1 << 20, vmem=VMEM_LIMIT):
    vm = pl.BlockSpec(memory_space=pltpu.VMEM)
    sm = pl.BlockSpec(memory_space=pltpu.SMEM)
    return pl.pallas_call(
        kernel,
        out_shape=outs,
        in_specs=[sm] * smem_in + [vm] * (len(args) - smem_in),
        out_specs=[sm] * smem_out + [vm] * (len(outs) - smem_out),
        scratch_shapes=list(scratch),
        compiler_params=pltpu.CompilerParams(vmem_limit_bytes=vmem),
        cost_estimate=pl.CostEstimate(flops=flops, bytes_accessed=1 << 20, transcendentals=0),
        name=name,
    )(*args)


def pack_kernel(q_ref, k_ref, v_ref, g_ref, doc_ref, out_ref):
    for pair in range(HEADS // 2):
        cols = slice(pair * 128, pair * 128 + 128)
        for a_ref, b_ref, at in ((q_ref, g_ref, 0), (k_ref, v_ref, ROWS)):
            a = a_ref[:, cols].astype(F32)
            b = b_ref[:, cols].astype(F32)
            low = lane_of(a) < HD
            out_ref[2 * pair, at : at + ROWS, :] = jnp.where(low, a, swap_halves(b)).astype(BF)
            out_ref[2 * pair + 1, at : at + ROWS, :] = jnp.where(low, swap_halves(a), b).astype(BF)
    group = lax.axis_index("zh") * 4 + lax.axis_index("x")
    docs = jnp.broadcast_to(doc_ref[...].astype(F32).reshape(1, 640), (16, 640))
    docs = pltpu.roll(docs, lax.rem(640 - group * ROWS, 640), 1)[:, 0:128].astype(BF)
    for h in range(HEADS):
        out_ref[h, 2 * ROWS : 2 * ROWS + 16, :] = docs


def swap_edges(ref, off):
    first = ref[0:16, :]
    last = ref[LONG : LONG + 16, :]
    early = row_of(first) < off
    ref[0:16, :] = jnp.where(early, last, first)
    ref[LONG : LONG + 16, :] = jnp.where(early, first, last)


def columns_of(doc_row):
    return jnp.broadcast_to(doc_row, (128, doc_row.shape[1])).T


def order_kernel(in_ref, at_ref, qg_ref, kv_ref, doc_ref):
    doc_at = slice(2 * ROWS, 2 * ROWS + 16)
    docs = jnp.concatenate([in_ref[b, doc_at, :].astype(F32)[0:1, :] for b in range(16)], axis=0)
    before = jnp.where((docs < docs[8:9, 0:1]) & (lane_of(docs) < ROWS), 1.0, 0.0)
    turned = jnp.concatenate([docs, jnp.zeros((112, 128), F32)], axis=0).T
    for b in range(16):
        doc_ref[OWN * 2 + b * ROWS : OWN * 2 + (b + 1) * ROWS, :] = jnp.broadcast_to(
            turned[0:ROWS, b : b + 1], (ROWS, 128)
        )
    start = jnp.sum(before).astype(jnp.int32)
    off = start & 15
    at_ref[0] = start - off
    at_ref[1] = off
    first = lax.shift_right_logical(start, 4)

    def place(i):
        at = first + i
        return at - jnp.where(at >= OWN // 16, OWN // 16, 0)

    def move(i, _):
        at = place(i)
        chunk = lax.shift_right_logical(at * 205, 10)
        part = (at - chunk * 5) * 16
        rows = pl.ds(pl.multiple_of(i * 16, 16), 16)
        qg_ref[rows, :] = in_ref[chunk, pl.ds(pl.multiple_of(part, 16), 16), :]
        kv_ref[rows, :] = in_ref[chunk, pl.ds(pl.multiple_of(ROWS + part, 16), 16), :]
        return 0

    lax.fori_loop(0, OWN // 16, move, 0, unroll=20)

    def move_docs(i, _):
        at = place(i) * 16
        rows = pl.ds(pl.multiple_of(i * 16, 16), 16)
        doc_ref[rows, :] = doc_ref[pl.ds(pl.multiple_of(OWN * 2 + at, 16), 16), :]
        return 0

    move_docs(0, 0)
    lax.fori_loop(LONG // 16, OWN // 16, move_docs, 0, unroll=4)
    for ref in (qg_ref, kv_ref, doc_ref):
        swap_edges(ref, off)
    docs = doc_ref[LONG : LONG + 384, :].T
    lines = [docs[0:1, n * 128 : n * 128 + 128] for n in range(3)]
    block = jnp.concatenate(lines + [jnp.zeros((13, 128), F32)], axis=0).astype(BF)
    qg_ref[OWN:SENT, :] = block
    kv_ref[OWN:SENT, :] = block


def doc_row_of(ref):
    lines = ref[OWN:SENT, :].astype(F32)
    return jnp.concatenate([lines[n : n + 1, :] for n in range(3)], axis=1)


def same_doc(doc_cols, doc_row):
    wide = jnp.concatenate([doc_cols] * (2 * REST // 128), axis=1)
    return (wide == doc_row)[0:REST, :]


def halves(x):
    zero = jnp.zeros_like(x)
    low = lane_of(x) < HD
    return jnp.where(low, x, zero), jnp.where(low, zero, x)


def totals_of(kv_refs, vet_ref, qg, grad_t, starts, mask_of, keep):
    q0, _ = halves(qg)
    scores, tops, outs = {}, [], []

    def finish(half, at, width):
        s = scores.pop((half, at))
        mask = mask_of(half) if mask_of else None
        if mask_of:
            s = jnp.where(mask, s, NEG)
        top = jnp.max(s, axis=0, keepdims=True) * LOG2_SCALE
        p = jnp.exp2(s * LOG2_SCALE - top)
        if mask_of:
            p = jnp.where(mask, p, 0.0)
        p = p.astype(BF)
        keep(half, at, p, top)
        lane = half * WIDE + lane_at(at)
        outs.append(dot_nn(vet_ref[:, lane : lane + width], p))
        tops.append(top)

    for n, (half, at, width) in enumerate(starts):
        scores[half, at] = dot_nt(kv_refs[half][at : at + width, :], q0)
        if n:
            finish(*starts[n - 1])
    finish(*starts[-1])
    top = functools.reduce(jnp.maximum, tops)
    shares = [jnp.exp2(t - top) for t in tops]
    total = sum(o[0:1, :] * w for o, w in zip(outs, shares))
    out = sum(o[HD:, :] * w for o, w in zip(outs, shares))
    dot = jnp.sum(out * grad_t.astype(F32), axis=0, keepdims=True)
    if mask_of:
        empty = total <= 0.0
        total = jnp.where(empty, 1.0, total)
        top = jnp.where(empty, NEG, top)
    return top + jnp.log2(total), dot / total


def lane_at(row):
    return row // STEP * 256


def prepare_keys(kv_refs, kvt_refs, vet_ref, col_ref):
    for half, (kv_ref, kvt_ref) in enumerate(zip(kv_refs, kvt_refs)):
        for at in (0, STEP, 2 * STEP, 3 * STEP, LONG):
            width = REST if at == LONG else STEP
            kvt_ref[:, lane_at(at) : lane_at(at) + width] = (
                kv_ref[at : at + width, :].T
            )
        kvt = kvt_ref[...]
        vet_ref[:, half * WIDE : (half + 1) * WIDE] = jnp.where(
            row_of(kvt) < HD, jnp.ones_like(kvt), kvt
        )
        col_ref[half] = columns_of(doc_row_of(kv_ref))


def rest_rows(first, second):
    return jnp.concatenate([first[LONG:OWN, :], second[LONG:OWN, :]], axis=0)


def totals(
    kv_refs, qg0, qg1, gt_ref, gt_rest_ref, stat_ref, kvt_refs, p_refs, rest_refs, top_refs,
    vet_ref, col_ref, qg_ref,
):
    prepare_keys(kv_refs, kvt_refs, vet_ref, col_ref)
    qg_ref[0] = qg0[0:LONG, :]
    qg_ref[1] = qg1[0:LONG, :]

    def block(n, _):
        def keep(half, at, p, top):
            p_refs[half][n, at : at + STEP, :] = p
            top_refs[half][n, at // STEP, :, 0:LONG] = top

        starts = [(half, at, STEP) for half in range(len(kv_refs)) for at in range(0, LONG, STEP)]
        lse, dot = totals_of(kv_refs, vet_ref, qg_ref[n], gt_ref[n], starts, None, keep)
        stat_ref[n, 0:1, 0:LONG] = lse
        stat_ref[n, 1:2, 0:LONG] = dot
        return 0

    for n in range(2):
        block(n, 0)

    def keep_rest(half, at, p, top):
        rest_refs[half][...] = p
        top_refs[half][2, 0, :, 0 : 2 * REST] = top

    doc_row = jnp.concatenate([doc_row_of(ref)[:, 0:REST] for ref in (qg0, qg1)], axis=1)
    lse, dot = totals_of(
        kv_refs,
        vet_ref,
        rest_rows(qg0, qg1),
        gt_rest_ref[...],
        [(half, LONG, REST) for half in range(len(kv_refs))],
        lambda half: same_doc(col_ref[half], doc_row),
        keep_rest,
    )
    stat_ref[2, 0:1, 0 : 2 * REST] = lse
    stat_ref[2, 1:2, 0 : 2 * REST] = dot


def added(pairs):
    top = functools.reduce(jnp.maximum, [lse for lse, _ in pairs])
    shares = [jnp.exp2(lse - top) for lse, _ in pairs]
    whole = sum(shares)
    return top + jnp.log2(whole), sum(w * dot for w, (_, dot) in zip(shares, pairs)) / whole


def own_totals_kernel(
    kv, qg0, qg1, stat_ref, gt_ref, gt_rest_ref, kvt, p, rest, top, *scratch
):
    for n, ref in enumerate((qg0, qg1)):
        gt_ref[n] = ref[0:LONG, :].T[HD:, :]
    gt_rest_ref[...] = rest_rows(qg0, qg1).T[HD:, :]
    totals([kv], qg0, qg1, gt_ref, gt_rest_ref, stat_ref, [kvt], [p], [rest], [top], *scratch)


def near_totals_kernel(kv1, kv3, qg0, qg1, gt_ref, gt_rest_ref, stat_ref, *refs):
    kvts, ps, rests, tops = (refs[2 * n : 2 * n + 2] for n in range(4))
    totals(
        [kv1, kv3], qg0, qg1, gt_ref, gt_rest_ref, stat_ref, kvts, ps, rests, tops, *refs[8:]
    )


def last_totals_kernel(
    kv, qg0, qg1, gt_ref, gt_rest_ref, first_ref, near_ref,
    stat_ref, kvt, p, rest, top, vet_ref, col_ref, qg_ref, last_ref,
):
    totals(
        [kv], qg0, qg1, gt_ref, gt_rest_ref, last_ref, [kvt], [p], [rest], [top],
        vet_ref, col_ref, qg_ref,
    )
    for n in range(3):
        parts = [(ref[n, 0:1, :], ref[n, 1:2, :]) for ref in (first_ref, near_ref, last_ref)]
        stat_ref[n, 0:1, :], stat_ref[n, 1:2, :] = added(parts)


def tile_grads(qg, starts, weights_of, dot, kv_ref, kvt_ref, dkv_ref):
    q0, g0 = halves(qg)
    acc = None
    for at, width in starts:
        kv = kv_ref[at : at + width, :]
        p = weights_of(at)
        ds = (p * (dot_nt(kv, g0) - dot)).astype(BF)
        dkv_ref[at : at + width, :] += dot_nn(p.astype(BF), g0) + dot_nn(ds, q0)
        part = dot_nn(kvt_ref[0:HD, lane_at(at) : lane_at(at) + width], ds)
        acc = part if acc is None else acc + part
    return acc


def packed_dq(dq):
    low = lax.broadcasted_iota(jnp.int32, (OWN // 2, 128), 1) < HD
    return jnp.where(low, dq[0 : OWN // 2, :], dq[OWN // 2 : OWN, :])


def grads_kernel(blocks, with_rest, names, *refs):
    ref = dict(zip(names, refs))
    dq_ref, dq_rest_ref, dkv_ref, row_ref = ref["dq"], ref["dq_rest"], ref["dkv"], ref["row"]
    kv_ref, kvt_ref, qg_ref = ref["kv"], ref["kvt"], ref["qg"]
    p_ref, rest_ref, top_ref = ref["p"], ref["rest"], ref["top"]
    if "rows" in ref:
        row_ref[...] = ref["rows"][...]
    else:
        for n in range(3):
            mine = [ref["stats"][n, k : k + 1, :] for k in range(2)]
            far = [ref["stats_far"][(1, 0, 2)[n], k : k + 1, :] for k in range(2)]
            if n == 2:
                far = [
                    jnp.concatenate([x[:, REST : 2 * REST], x[:, 0:REST], x[:, 2 * REST :]], axis=1)
                    for x in far
                ]
            row_ref[n, 0:1, :], row_ref[n, 1:2, :] = added([mine, far])
        ref["rows_out"][...] = row_ref[...]
    for n in range(2):
        qg_ref[n] = ref["qg", n][0:LONG, :]
    for out, known in ((dq_ref, "dq_in"), (dq_rest_ref, "dq_rest_in")):
        out[...] = ref[known][...] if known in ref else jnp.zeros_like(out)
    dkv_ref[...] = ref["dkv_in"][...] if "dkv_in" in ref else jnp.zeros_like(dkv_ref)

    def block(n, _):
        lse = row_ref[n, 0:1, 0:LONG]

        def weights_of(at):
            share = jnp.exp2(top_ref[n, at // STEP, :, 0:LONG] - lse)
            return p_ref[n, at : at + STEP, :].astype(F32) * share

        starts = [(at, STEP) for at in range(0, LONG, STEP)]
        dot = row_ref[n, 1:2, 0:LONG]
        dq_ref[n] += tile_grads(qg_ref[n], starts, weights_of, dot, kv_ref, kvt_ref, dkv_ref)
        return 0

    for n in blocks:
        block(n, 0)
    if with_rest:
        both = slice(0, 2 * REST)
        share = jnp.exp2(top_ref[2, 0, :, both] - row_ref[2, 0:1, both])
        dq_rest_ref[...] += tile_grads(
            rest_rows(ref["qg", 0], ref["qg", 1]),
            [(LONG, REST)],
            lambda at: rest_ref[...].astype(F32) * share,
            row_ref[2, 1:2, both],
            kv_ref,
            kvt_ref,
            dkv_ref,
        )
    if "dkv_out" in ref:
        ref["dkv_out"][...] = dkv_ref[...]
    if "dkv_send" in ref:
        relay = ref["relay"][...].astype(F32) if "relay" in ref else 0.0
        ref["dkv_send"][...] = (dkv_ref[...] + relay).astype(BF)
    for n, (whole, name) in enumerate((("dq_out", "dq_out"), ("dq_send", "dq_rows"))):
        if whole in ref:
            rest = dq_rest_ref[:, n * REST : (n + 1) * REST] * SCALE
            ref[name][0:LONG, :] = jnp.concatenate([dq_ref[n] * SCALE] * 2, axis=0).T
            ref[name][LONG:OWN, :] = jnp.concatenate([rest] * 2, axis=0).T
    if "dq_send" in ref:
        ref["dq_send"][...] = packed_dq(ref["dq_rows"][...]).astype(BF)


def grads(name, keys, arrays, takes, gives, blocks=(0, 1), with_rest=True):
    arrays.update(keys)
    ins = [*keys, ("qg", 0), ("qg", 1), *takes]
    shapes = {
        "dq": shape(2, HD, LONG, dtype=F32),
        "dq_rest": shape(HD, 2 * REST, dtype=F32),
        "dkv_send": shape(OWN, 128),
        "dq_send": shape(OWN // 2, 128),
        "rows_out": shape(3, 2, 1024, dtype=F32),
    }
    scratch = dict(
        dkv=pltpu.VMEM((OWN, 128), F32),
        row=pltpu.VMEM((3, 2, 1024), F32),
        qg=pltpu.VMEM((2, LONG, 128), BF),
    )
    if "dq" not in gives:
        scratch["dq"] = pltpu.VMEM((2, HD, LONG), F32)
    if "dq_rest" not in gives:
        scratch["dq_rest"] = pltpu.VMEM((HD, 2 * REST), F32)
    if "dq_send" in gives:
        scratch["dq_rows"] = pltpu.VMEM((OWN, 128), F32)
    results = call(
        functools.partial(grads_kernel, blocks, with_rest, ins + list(gives) + list(scratch)),
        name,
        [shapes[g] if g in shapes else shape(OWN, 128, dtype=F32) for g in gives],
        [arrays[n] for n in ins],
        scratch=scratch.values(),
        flops=3_000_000_000 * len(blocks),
    )
    arrays.update(zip(gives, results))


def merge_kernel(at_ref, own_dq, far_dq, own_dkv, dkv1, dkv3, out_ref, dq_ref, dkv_ref):
    half = OWN // 2
    far = far_dq[...].astype(F32)
    turned = swap_halves(far)
    low = lane_of(far) < HD
    dq_ref[0:half, :] = own_dq[0:half, :] + jnp.where(low, far, turned)
    dq_ref[half:OWN, :] = own_dq[half:OWN, :] + jnp.where(low, turned, far)
    dkv = own_dkv[...] + sum(ref[...].astype(F32) for ref in (dkv1, dkv3))
    dkv_ref[...] = jnp.where(lane_of(dkv) < HD, dkv * SCALE, dkv)
    off = at_ref[1]
    swap_edges(dq_ref, off)
    swap_edges(dkv_ref, off)
    base = at_ref[0]

    def chunk(c, _):
        def sixteen(ref, n):
            spot = c * ROWS + 16 * n - base
            spot = spot + jnp.where(spot < 0, OWN, 0)
            return ref[pl.ds(pl.multiple_of(spot, 16), 16), :]

        for n in range(5):
            out_ref[c, 16 * n : 16 * n + 16, :] = sixteen(dkv_ref, n).astype(BF)
        groups = [sixteen(dq_ref, n) for n in range(5)]
        low = lane_of(groups[0]) < HD
        out_ref[c, 80:96, :] = jnp.where(low, groups[0], groups[1]).astype(BF)
        out_ref[c, 96:112, :] = jnp.where(low, groups[2], groups[3]).astype(BF)
        out_ref[c, 112:128, :] = groups[4].astype(BF)
        return 0

    lax.fori_loop(0, 16, chunk, 0, unroll=8)


def join_kernel(in_ref, q_out, k_out, v_out):
    for pair in range(HEADS // 2):
        cols = slice(pair * 128, pair * 128 + 128)
        a, b = in_ref[2 * pair].astype(F32), in_ref[2 * pair + 1].astype(F32)
        a_swap, b_swap = swap_halves(a), swap_halves(b)
        low = lane_of(a) < HD
        even, odd = jnp.where(low, a, b_swap).astype(BF), jnp.where(low, a_swap, b).astype(BF)
        k_out[:, cols] = even[0:ROWS]
        v_out[:, cols] = odd[0:ROWS]
        for n in range(5):
            part = slice(ROWS + 16 * (n // 2), ROWS + 16 * (n // 2) + 16)
            q_out[16 * n : 16 * n + 16, cols] = (odd if n % 2 else even)[part]


def shifted(array, by):
    pairs = [
        (c * 4 + x, c * 4 + (x + (by if c == 0 else -by)) % 4) for c in range(2) for x in range(4)
    ]
    return lax.ppermute(array, ("c", "x"), pairs)


def crossed(array):
    return lax.ppermute(array, "c", [(0, 1), (1, 0)])


def body(queries, keys, values, out_grad, doc_ids):
    packed = call(
        pack_kernel,
        "pack",
        [shape(16, 176, 128)],
        [queries, keys, values, out_grad, doc_ids],
        vmem=56 << 20,
    )[0]
    packed = lax.all_to_all(packed, BY_HEAD, 0, 0, tiled=True)
    at, qg, kv = call(
        order_kernel,
        "order",
        [shape(2, dtype=jnp.int32), shape(SENT, 128), shape(SENT, 128)],
        [packed],
        smem_out=1,
        scratch=[pltpu.VMEM((3 * OWN, 128), F32)],
    )
    qg_far = crossed(qg)
    kv1, kv3 = shifted(kv, 1), shifted(kv, -1)

    def side(sets):
        return [
            pltpu.VMEM((128, sets * WIDE), BF),
            pltpu.VMEM((sets, 384, 128), F32),
            pltpu.VMEM((2, LONG, 128), BF),
        ]

    stat, turned = shape(3, 2, 1024, dtype=F32), shape(128, WIDE)
    kept, kept_rest = shape(2, LONG, LONG), shape(REST, 2 * REST)
    kept_top = shape(3, LONG // STEP, 1, 1024, dtype=F32)
    grad_t = [shape(2, HD, LONG), shape(HD, 2 * REST)]
    first, *grad_t, kvt0, p0, rest0, top0 = call(
        own_totals_kernel,
        "totals_own",
        [stat, *grad_t, turned, kept, kept_rest, kept_top],
        [kv, qg, qg_far],
        scratch=side(1),
        flops=2_500_000_000,
    )
    kv1, first = lax.optimization_barrier((kv1, first))
    kv2 = shifted(kv1, 1)
    near, kvt1, kvt3, p1, p3, rest1, rest3, top1, top3 = call(
        near_totals_kernel,
        "totals_near",
        [stat] + [turned] * 2 + [kept] * 2 + [kept_rest] * 2 + [kept_top] * 2,
        [kv1, kv3, qg, qg_far, *grad_t],
        scratch=side(2),
        flops=5_000_000_000,
    )
    stats, kvt2, p2, rest2, top2 = call(
        last_totals_kernel,
        "totals_far",
        [stat, turned, kept, kept_rest, kept_top],
        [kv2, qg, qg_far, *grad_t, first, near],
        scratch=side(1) + [pltpu.VMEM((3, 2, 1024), F32)],
        flops=2_500_000_000,
    )

    sets = [
        dict(zip(("kv", "kvt", "p", "rest", "top"), one))
        for one in (
            (kv, kvt0, p0, rest0, top0),
            (kv1, kvt1, p1, rest1, top1),
            (kv2, kvt2, p2, rest2, top2),
            (kv3, kvt3, p3, rest3, top3),
        )
    ]
    arrays = {("qg", 0): qg, ("qg", 1): qg_far, "stats": stats, "stats_far": crossed(stats)}
    takes, gives = ["stats", "stats_far"], ["rows_out", "dq", "dq_rest", "dkv_send"]
    sent = {}
    for name, n, by in (("grads_far", 2, 1), ("grads_one", 1, -1), ("grads_three", 3, 1)):
        grads(name, sets[n], arrays, takes, gives)
        arrays["rows"] = arrays["rows_out"]
        arrays["dq_in"], arrays["dq_rest_in"] = arrays["dq"], arrays["dq_rest"]
        takes, gives = ["rows", "dq_in", "dq_rest_in"], ["dq", "dq_rest", "dkv_send"]
        sent[n] = shifted(arrays["dkv_send"], by)
        if n == 1:
            arrays["relay"] = sent[2]
            takes = [*takes, "relay"]
    takes = ["rows", "dq_in", "dq_rest_in"]
    gives = ["dq_send", "dq_rest", "dkv_out"]
    grads("grads_own_far", sets[0], arrays, takes, gives, blocks=(1,))
    far_dq = crossed(arrays["dq_send"])
    arrays["dkv_in"], arrays["dq_rest_in"] = arrays["dkv_out"], arrays["dq_rest"]
    sent[1], arrays["dq_in"] = lax.optimization_barrier((sent[1], arrays["dq_in"]))
    grads(
        "grads_own", sets[0], arrays, [*takes, "dkv_in"], ["dq_out", "dkv_out"], (0,), False
    )
    merged = call(
        merge_kernel,
        "merge",
        [shape(16, 128, 128)],
        [at, arrays["dq_out"], far_dq, arrays["dkv_out"], sent[1], sent[3]],
        smem_in=1,
        scratch=[pltpu.VMEM((OWN, 128), F32), pltpu.VMEM((OWN, 128), F32)],
    )[0]
    merged = lax.all_to_all(merged, BY_HEAD, 0, 0, tiled=True)
    return tuple(call(join_kernel, "join", [shape(ROWS, HEADS * HD)] * 3, [merged]))


def solution(mesh):
    fine = Mesh(mesh.devices.reshape(4, 2, 2, 2, 4), BLK + ("zh", "x"))
    rows = P(BLK + ("zh", "x"), None)
    return jax.shard_map(
        body,
        mesh=fine,
        in_specs=(rows, rows, rows, rows, P(BLK)),
        out_specs=(rows, rows, rows),
        check_vma=False,
    )
```

```python
import functools
import math

import jax
import jax.numpy as jnp
from jax import lax
from jax.experimental import pallas as pl
from jax.experimental.pallas import tpu as pltpu
from jax.sharding import Mesh
from jax.sharding import PartitionSpec as P

BF = jnp.bfloat16
F32 = jnp.float32
HD = 64
HEADS = 16
ROWS = 80
OWN = 1280
LONG = 960
REST = OWN - LONG
SENT = OWN + 16
STEP = 240
WIDE = 1408
SCALE = 1.0 / math.sqrt(HD)
LOG2_SCALE = SCALE * math.log2(math.e)
NEG = -1e30
BLK = ("y", "zl", "c")
BY_HEAD = ("y", "zl", "zh")
VMEM_LIMIT = 24 << 20


def dot_nt(a, b):
    return lax.dot_general(a, b, (((1,), (1,)), ((), ())), preferred_element_type=F32)


def dot_nn(a, b):
    return lax.dot_general(a, b, (((1,), (0,)), ((), ())), preferred_element_type=F32)


def lane_of(x):
    return lax.broadcasted_iota(jnp.int32, x.shape, x.ndim - 1)


def row_of(x):
    return lax.broadcasted_iota(jnp.int32, x.shape, 0)


def swap_halves(x):
    return pltpu.roll(x, HD, 1)


def shape(*dims, dtype=BF):
    return jax.ShapeDtypeStruct(dims, dtype)


def call(kernel, name, outs, args, smem_in=0, smem_out=0, scratch=(), flops=1 << 20, vmem=VMEM_LIMIT):
    vm = pl.BlockSpec(memory_space=pltpu.VMEM)
    sm = pl.BlockSpec(memory_space=pltpu.SMEM)
    return pl.pallas_call(
        kernel,
        out_shape=outs,
        in_specs=[sm] * smem_in + [vm] * (len(args) - smem_in),
        out_specs=[sm] * smem_out + [vm] * (len(outs) - smem_out),
        scratch_shapes=list(scratch),
        compiler_params=pltpu.CompilerParams(vmem_limit_bytes=vmem),
        cost_estimate=pl.CostEstimate(flops=flops, bytes_accessed=1 << 20, transcendentals=0),
        name=name,
    )(*args)


def pack_kernel(q_ref, k_ref, v_ref, g_ref, doc_ref, out_ref):
    for pair in range(HEADS // 2):
        cols = slice(pair * 128, pair * 128 + 128)
        for a_ref, b_ref, at in ((q_ref, g_ref, 0), (k_ref, v_ref, ROWS)):
            a = a_ref[:, cols].astype(F32)
            b = b_ref[:, cols].astype(F32)
            low = lane_of(a) < HD
            out_ref[2 * pair, at : at + ROWS, :] = jnp.where(low, a, swap_halves(b)).astype(BF)
            out_ref[2 * pair + 1, at : at + ROWS, :] = jnp.where(low, swap_halves(a), b).astype(BF)
    group = lax.axis_index("zh") * 4 + lax.axis_index("x")
    docs = jnp.broadcast_to(doc_ref[...].astype(F32).reshape(1, 640), (16, 640))
    docs = pltpu.roll(docs, lax.rem(640 - group * ROWS, 640), 1)[:, 0:128].astype(BF)
    for h in range(HEADS):
        out_ref[h, 2 * ROWS : 2 * ROWS + 16, :] = docs


def swap_edges(ref, off):
    first = ref[0:16, :]
    last = ref[LONG : LONG + 16, :]
    early = row_of(first) < off
    ref[0:16, :] = jnp.where(early, last, first)
    ref[LONG : LONG + 16, :] = jnp.where(early, first, last)


def columns_of(doc_row):
    return jnp.broadcast_to(doc_row, (128, doc_row.shape[1])).T


def order_kernel(in_ref, at_ref, qg_ref, kv_ref, doc_ref):
    doc_at = slice(2 * ROWS, 2 * ROWS + 16)
    docs = jnp.concatenate([in_ref[b, doc_at, :].astype(F32)[0:1, :] for b in range(16)], axis=0)
    before = jnp.where((docs < docs[8:9, 0:1]) & (lane_of(docs) < ROWS), 1.0, 0.0)
    turned = jnp.concatenate([docs, jnp.zeros((112, 128), F32)], axis=0).T
    for b in range(16):
        doc_ref[OWN * 2 + b * ROWS : OWN * 2 + (b + 1) * ROWS, :] = jnp.broadcast_to(
            turned[0:ROWS, b : b + 1], (ROWS, 128)
        )
    start = jnp.sum(before).astype(jnp.int32)
    off = start & 15
    at_ref[0] = start - off
    at_ref[1] = off
    first = lax.shift_right_logical(start, 4)

    def place(i):
        at = first + i
        return at - jnp.where(at >= OWN // 16, OWN // 16, 0)

    def move(i, _):
        at = place(i)
        chunk = lax.shift_right_logical(at * 205, 10)
        part = (at - chunk * 5) * 16
        rows = pl.ds(pl.multiple_of(i * 16, 16), 16)
        qg_ref[rows, :] = in_ref[chunk, pl.ds(pl.multiple_of(part, 16), 16), :]
        kv_ref[rows, :] = in_ref[chunk, pl.ds(pl.multiple_of(ROWS + part, 16), 16), :]
        return 0

    lax.fori_loop(0, OWN // 16, move, 0, unroll=20)

    def move_docs(i, _):
        at = place(i) * 16
        rows = pl.ds(pl.multiple_of(i * 16, 16), 16)
        doc_ref[rows, :] = doc_ref[pl.ds(pl.multiple_of(OWN * 2 + at, 16), 16), :]
        return 0

    move_docs(0, 0)
    lax.fori_loop(LONG // 16, OWN // 16, move_docs, 0, unroll=4)
    for ref in (qg_ref, kv_ref, doc_ref):
        swap_edges(ref, off)
    docs = doc_ref[LONG : LONG + 384, :].T
    lines = [docs[0:1, n * 128 : n * 128 + 128] for n in range(3)]
    block = jnp.concatenate(lines + [jnp.zeros((13, 128), F32)], axis=0).astype(BF)
    qg_ref[OWN:SENT, :] = block
    kv_ref[OWN:SENT, :] = block


def doc_row_of(ref):
    lines = ref[OWN:SENT, :].astype(F32)
    return jnp.concatenate([lines[n : n + 1, :] for n in range(3)], axis=1)


def same_doc(doc_cols, doc_row):
    wide = jnp.concatenate([doc_cols] * (2 * REST // 128), axis=1)
    return (wide == doc_row)[0:REST, :]


def halves(x):
    zero = jnp.zeros_like(x)
    low = lane_of(x) < HD
    return jnp.where(low, x, zero), jnp.where(low, zero, x)


def totals_of(kv_refs, vet_ref, qg, grad_t, starts, mask_of, keep):
    q0, _ = halves(qg)
    scores, tops, outs = {}, [], []

    def finish(half, at, width):
        s = scores.pop((half, at))
        mask = mask_of(half) if mask_of else None
        if mask_of:
            s = jnp.where(mask, s, NEG)
        top = jnp.max(s, axis=0, keepdims=True) * LOG2_SCALE
        p = jnp.exp2(s * LOG2_SCALE - top)
        if mask_of:
            p = jnp.where(mask, p, 0.0)
        p = p.astype(BF)
        keep(half, at, p, top)
        lane = half * WIDE + lane_at(at)
        outs.append(dot_nn(vet_ref[:, lane : lane + width], p))
        tops.append(top)

    for n, (half, at, width) in enumerate(starts):
        scores[half, at] = dot_nt(kv_refs[half][at : at + width, :], q0)
        if n:
            finish(*starts[n - 1])
    finish(*starts[-1])
    top = functools.reduce(jnp.maximum, tops)
    shares = [jnp.exp2(t - top) for t in tops]
    total = sum(o[0:1, :] * w for o, w in zip(outs, shares))
    out = sum(o[HD:, :] * w for o, w in zip(outs, shares))
    dot = jnp.sum(out * grad_t.astype(F32), axis=0, keepdims=True)
    if mask_of:
        empty = total <= 0.0
        total = jnp.where(empty, 1.0, total)
        top = jnp.where(empty, NEG, top)
    return top + jnp.log2(total), dot / total


def lane_at(row):
    return row // STEP * 256


def prepare_keys(kv_refs, kvt_refs, vet_ref, col_ref):
    for half, (kv_ref, kvt_ref) in enumerate(zip(kv_refs, kvt_refs)):
        for at in (0, STEP, 2 * STEP, 3 * STEP, LONG):
            width = REST if at == LONG else STEP
            kvt_ref[:, lane_at(at) : lane_at(at) + width] = (
                kv_ref[at : at + width, :].T
            )
        kvt = kvt_ref[...]
        vet_ref[:, half * WIDE : (half + 1) * WIDE] = jnp.where(
            row_of(kvt) < HD, jnp.ones_like(kvt), kvt
        )
        col_ref[half] = columns_of(doc_row_of(kv_ref))


def rest_rows(first, second):
    return jnp.concatenate([first[LONG:OWN, :], second[LONG:OWN, :]], axis=0)


def totals(
    kv_refs, qg0, qg1, gt_ref, gt_rest_ref, stat_ref, kvt_refs, p_refs, rest_refs, top_refs,
    vet_ref, col_ref, qg_ref,
):
    prepare_keys(kv_refs, kvt_refs, vet_ref, col_ref)
    qg_ref[0] = qg0[0:LONG, :]
    qg_ref[1] = qg1[0:LONG, :]

    def block(n, _):
        def keep(half, at, p, top):
            p_refs[half][n, at : at + STEP, :] = p
            top_refs[half][n, at // STEP, :, 0:LONG] = top

        starts = [(half, at, STEP) for half in range(len(kv_refs)) for at in range(0, LONG, STEP)]
        lse, dot = totals_of(kv_refs, vet_ref, qg_ref[n], gt_ref[n], starts, None, keep)
        stat_ref[n, 0:1, 0:LONG] = lse
        stat_ref[n, 1:2, 0:LONG] = dot
        return 0

    for n in range(2):
        block(n, 0)

    def keep_rest(half, at, p, top):
        rest_refs[half][...] = p
        top_refs[half][2, 0, :, 0 : 2 * REST] = top

    doc_row = jnp.concatenate([doc_row_of(ref)[:, 0:REST] for ref in (qg0, qg1)], axis=1)
    lse, dot = totals_of(
        kv_refs,
        vet_ref,
        rest_rows(qg0, qg1),
        gt_rest_ref[...],
        [(half, LONG, REST) for half in range(len(kv_refs))],
        lambda half: same_doc(col_ref[half], doc_row),
        keep_rest,
    )
    stat_ref[2, 0:1, 0 : 2 * REST] = lse
    stat_ref[2, 1:2, 0 : 2 * REST] = dot


def added(pairs):
    top = functools.reduce(jnp.maximum, [lse for lse, _ in pairs])
    shares = [jnp.exp2(lse - top) for lse, _ in pairs]
    whole = sum(shares)
    return top + jnp.log2(whole), sum(w * dot for w, (_, dot) in zip(shares, pairs)) / whole


def own_totals_kernel(
    kv, qg0, qg1, stat_ref, gt_ref, gt_rest_ref, kvt, p, rest, top, prob_grad_ref, *scratch
):
    for n, ref in enumerate((qg0, qg1)):
        gt_ref[n] = ref[0:LONG, :].T[HD:, :]
        _, g0 = halves(ref[0:LONG, :])
        for at in range(0, LONG, STEP):
            prob_grad_ref[n, at : at + STEP, :] = dot_nt(kv[at : at + STEP, :], g0)
    gt_rest_ref[...] = rest_rows(qg0, qg1).T[HD:, :]
    totals([kv], qg0, qg1, gt_ref, gt_rest_ref, stat_ref, [kvt], [p], [rest], [top], *scratch)


def near_totals_kernel(kv1, kv3, qg0, qg1, gt_ref, gt_rest_ref, stat_ref, *refs):
    kvts, ps, rests, tops = (refs[2 * n : 2 * n + 2] for n in range(4))
    totals(
        [kv1, kv3], qg0, qg1, gt_ref, gt_rest_ref, stat_ref, kvts, ps, rests, tops, *refs[8:]
    )


def last_totals_kernel(
    kv, qg0, qg1, gt_ref, gt_rest_ref, first_ref, near_ref,
    stat_ref, kvt, p, rest, top, vet_ref, col_ref, qg_ref, last_ref,
):
    totals(
        [kv], qg0, qg1, gt_ref, gt_rest_ref, last_ref, [kvt], [p], [rest], [top],
        vet_ref, col_ref, qg_ref,
    )
    for n in range(3):
        parts = [(ref[n, 0:1, :], ref[n, 1:2, :]) for ref in (first_ref, near_ref, last_ref)]
        stat_ref[n, 0:1, :], stat_ref[n, 1:2, :] = added(parts)


def tile_grads(qg, starts, weights_of, dot, kv_ref, kvt_ref, dkv_ref, prob_grad_of=None):
    q0, g0 = halves(qg)
    acc = None
    for at, width in starts:
        kv = kv_ref[at : at + width, :]
        p = weights_of(at)
        prob_grad = prob_grad_of(at) if prob_grad_of else dot_nt(kv, g0)
        ds = (p * (prob_grad - dot)).astype(BF)
        dkv_ref[at : at + width, :] += dot_nn(p.astype(BF), g0) + dot_nn(ds, q0)
        part = dot_nn(kvt_ref[0:HD, lane_at(at) : lane_at(at) + width], ds)
        acc = part if acc is None else acc + part
    return acc


def packed_dq(dq):
    low = lax.broadcasted_iota(jnp.int32, (OWN // 2, 128), 1) < HD
    return jnp.where(low, dq[0 : OWN // 2, :], dq[OWN // 2 : OWN, :])


def grads_kernel(blocks, with_rest, names, *refs):
    ref = dict(zip(names, refs))
    dq_ref, dq_rest_ref, dkv_ref, row_ref = ref["dq"], ref["dq_rest"], ref["dkv"], ref["row"]
    kv_ref, kvt_ref, qg_ref = ref["kv"], ref["kvt"], ref["qg"]
    p_ref, rest_ref, top_ref = ref["p"], ref["rest"], ref["top"]
    if "rows" in ref:
        row_ref[...] = ref["rows"][...]
    else:
        for n in range(3):
            mine = [ref["stats"][n, k : k + 1, :] for k in range(2)]
            far = [ref["stats_far"][(1, 0, 2)[n], k : k + 1, :] for k in range(2)]
            if n == 2:
                far = [
                    jnp.concatenate([x[:, REST : 2 * REST], x[:, 0:REST], x[:, 2 * REST :]], axis=1)
                    for x in far
                ]
            row_ref[n, 0:1, :], row_ref[n, 1:2, :] = added([mine, far])
        ref["rows_out"][...] = row_ref[...]
    for n in range(2):
        qg_ref[n] = ref["qg", n][0:LONG, :]
    for out, known in ((dq_ref, "dq_in"), (dq_rest_ref, "dq_rest_in")):
        out[...] = ref[known][...] if known in ref else jnp.zeros_like(out)
    dkv_ref[...] = ref["dkv_in"][...] if "dkv_in" in ref else jnp.zeros_like(dkv_ref)

    def block(n, _):
        lse = row_ref[n, 0:1, 0:LONG]

        def weights_of(at):
            share = jnp.exp2(top_ref[n, at // STEP, :, 0:LONG] - lse)
            return p_ref[n, at : at + STEP, :].astype(F32) * share

        starts = [(at, STEP) for at in range(0, LONG, STEP)]
        dot = row_ref[n, 1:2, 0:LONG]
        prob_grad_of = None
        if "prob_grad" in ref:
            prob_grad_of = lambda at: ref["prob_grad"][n, at : at + STEP, :]
        dq_ref[n] += tile_grads(
            qg_ref[n], starts, weights_of, dot, kv_ref, kvt_ref, dkv_ref, prob_grad_of
        )
        return 0

    for n in blocks:
        block(n, 0)
    if with_rest:
        both = slice(0, 2 * REST)
        share = jnp.exp2(top_ref[2, 0, :, both] - row_ref[2, 0:1, both])
        dq_rest_ref[...] += tile_grads(
            rest_rows(ref["qg", 0], ref["qg", 1]),
            [(LONG, REST)],
            lambda at: rest_ref[...].astype(F32) * share,
            row_ref[2, 1:2, both],
            kv_ref,
            kvt_ref,
            dkv_ref,
        )
    if "dkv_out" in ref:
        ref["dkv_out"][...] = dkv_ref[...]
    if "dkv_send" in ref:
        relay = ref["relay"][...].astype(F32) if "relay" in ref else 0.0
        ref["dkv_send"][...] = (dkv_ref[...] + relay).astype(BF)
    for n, (whole, name) in enumerate((("dq_out", "dq_out"), ("dq_send", "dq_rows"))):
        if whole in ref:
            rest = dq_rest_ref[:, n * REST : (n + 1) * REST] * SCALE
            ref[name][0:LONG, :] = jnp.concatenate([dq_ref[n] * SCALE] * 2, axis=0).T
            ref[name][LONG:OWN, :] = jnp.concatenate([rest] * 2, axis=0).T
    if "dq_send" in ref:
        ref["dq_send"][...] = packed_dq(ref["dq_rows"][...]).astype(BF)


def grads(name, keys, arrays, takes, gives, blocks=(0, 1), with_rest=True):
    arrays.update(keys)
    ins = [*keys, ("qg", 0), ("qg", 1), *takes]
    shapes = {
        "dq": shape(2, HD, LONG, dtype=F32),
        "dq_rest": shape(HD, 2 * REST, dtype=F32),
        "dkv_send": shape(OWN, 128),
        "dq_send": shape(OWN // 2, 128),
        "rows_out": shape(3, 2, 1024, dtype=F32),
    }
    scratch = dict(
        dkv=pltpu.VMEM((OWN, 128), F32),
        row=pltpu.VMEM((3, 2, 1024), F32),
        qg=pltpu.VMEM((2, LONG, 128), BF),
    )
    if "dq" not in gives:
        scratch["dq"] = pltpu.VMEM((2, HD, LONG), F32)
    if "dq_rest" not in gives:
        scratch["dq_rest"] = pltpu.VMEM((HD, 2 * REST), F32)
    if "dq_send" in gives:
        scratch["dq_rows"] = pltpu.VMEM((OWN, 128), F32)
    results = call(
        functools.partial(grads_kernel, blocks, with_rest, ins + list(gives) + list(scratch)),
        name,
        [shapes[g] if g in shapes else shape(OWN, 128, dtype=F32) for g in gives],
        [arrays[n] for n in ins],
        scratch=scratch.values(),
        flops=3_000_000_000 * len(blocks),
    )
    arrays.update(zip(gives, results))


def merge_kernel(at_ref, own_dq, far_dq, own_dkv, dkv1, dkv3, out_ref, dq_ref, dkv_ref):
    half = OWN // 2
    far = far_dq[...].astype(F32)
    turned = swap_halves(far)
    low = lane_of(far) < HD
    dq_ref[0:half, :] = own_dq[0:half, :] + jnp.where(low, far, turned)
    dq_ref[half:OWN, :] = own_dq[half:OWN, :] + jnp.where(low, turned, far)
    dkv = own_dkv[...] + sum(ref[...].astype(F32) for ref in (dkv1, dkv3))
    dkv_ref[...] = jnp.where(lane_of(dkv) < HD, dkv * SCALE, dkv)
    off = at_ref[1]
    swap_edges(dq_ref, off)
    swap_edges(dkv_ref, off)
    base = at_ref[0]

    def chunk(c, _):
        def sixteen(ref, n):
            spot = c * ROWS + 16 * n - base
            spot = spot + jnp.where(spot < 0, OWN, 0)
            return ref[pl.ds(pl.multiple_of(spot, 16), 16), :]

        for n in range(5):
            out_ref[c, 16 * n : 16 * n + 16, :] = sixteen(dkv_ref, n).astype(BF)
        groups = [sixteen(dq_ref, n) for n in range(5)]
        low = lane_of(groups[0]) < HD
        out_ref[c, 80:96, :] = jnp.where(low, groups[0], groups[1]).astype(BF)
        out_ref[c, 96:112, :] = jnp.where(low, groups[2], groups[3]).astype(BF)
        out_ref[c, 112:128, :] = groups[4].astype(BF)
        return 0

    lax.fori_loop(0, 16, chunk, 0, unroll=8)


def join_kernel(in_ref, q_out, k_out, v_out):
    for pair in range(HEADS // 2):
        cols = slice(pair * 128, pair * 128 + 128)
        a, b = in_ref[2 * pair].astype(F32), in_ref[2 * pair + 1].astype(F32)
        a_swap, b_swap = swap_halves(a), swap_halves(b)
        low = lane_of(a) < HD
        even, odd = jnp.where(low, a, b_swap).astype(BF), jnp.where(low, a_swap, b).astype(BF)
        k_out[:, cols] = even[0:ROWS]
        v_out[:, cols] = odd[0:ROWS]
        for n in range(5):
            part = slice(ROWS + 16 * (n // 2), ROWS + 16 * (n // 2) + 16)
            q_out[16 * n : 16 * n + 16, cols] = (odd if n % 2 else even)[part]


def shifted(array, by):
    pairs = [
        (c * 4 + x, c * 4 + (x + (by if c == 0 else -by)) % 4) for c in range(2) for x in range(4)
    ]
    return lax.ppermute(array, ("c", "x"), pairs)


def crossed(array):
    return lax.ppermute(array, "c", [(0, 1), (1, 0)])


def body(queries, keys, values, out_grad, doc_ids):
    packed = call(
        pack_kernel,
        "pack",
        [shape(16, 176, 128)],
        [queries, keys, values, out_grad, doc_ids],
        vmem=56 << 20,
    )[0]
    packed = lax.all_to_all(packed, BY_HEAD, 0, 0, tiled=True)
    at, qg, kv = call(
        order_kernel,
        "order",
        [shape(2, dtype=jnp.int32), shape(SENT, 128), shape(SENT, 128)],
        [packed],
        smem_out=1,
        scratch=[pltpu.VMEM((3 * OWN, 128), F32)],
    )
    qg_far = crossed(qg)
    kv1, kv3 = shifted(kv, 1), shifted(kv, -1)

    def side(sets):
        return [
            pltpu.VMEM((128, sets * WIDE), BF),
            pltpu.VMEM((sets, 384, 128), F32),
            pltpu.VMEM((2, LONG, 128), BF),
        ]

    stat, turned = shape(3, 2, 1024, dtype=F32), shape(128, WIDE)
    kept, kept_rest = shape(2, LONG, LONG), shape(REST, 2 * REST)
    kept_top = shape(3, LONG // STEP, 1, 1024, dtype=F32)
    grad_t = [shape(2, HD, LONG), shape(HD, 2 * REST)]
    first, *grad_t, kvt0, p0, rest0, top0, prob_grad = call(
        own_totals_kernel,
        "totals_own",
        [stat, *grad_t, turned, kept, kept_rest, kept_top, shape(2, LONG, LONG, dtype=F32)],
        [kv, qg, qg_far],
        scratch=side(1),
        flops=2_500_000_000,
    )
    kv1, first = lax.optimization_barrier((kv1, first))
    kv2 = shifted(kv1, 1)
    near, kvt1, kvt3, p1, p3, rest1, rest3, top1, top3 = call(
        near_totals_kernel,
        "totals_near",
        [stat] + [turned] * 2 + [kept] * 2 + [kept_rest] * 2 + [kept_top] * 2,
        [kv1, kv3, qg, qg_far, *grad_t],
        scratch=side(2),
        flops=5_000_000_000,
    )
    stats, kvt2, p2, rest2, top2 = call(
        last_totals_kernel,
        "totals_far",
        [stat, turned, kept, kept_rest, kept_top],
        [kv2, qg, qg_far, *grad_t, first, near],
        scratch=side(1) + [pltpu.VMEM((3, 2, 1024), F32)],
        flops=2_500_000_000,
    )

    sets = [
        dict(zip(("kv", "kvt", "p", "rest", "top"), one))
        for one in (
            (kv, kvt0, p0, rest0, top0),
            (kv1, kvt1, p1, rest1, top1),
            (kv2, kvt2, p2, rest2, top2),
            (kv3, kvt3, p3, rest3, top3),
        )
    ]
    arrays = {("qg", 0): qg, ("qg", 1): qg_far, "stats": stats, "stats_far": crossed(stats)}
    takes, gives = ["stats", "stats_far"], ["rows_out", "dq", "dq_rest", "dkv_send"]
    sent = {}
    for name, n, by in (("grads_far", 2, 1), ("grads_one", 1, -1), ("grads_three", 3, 1)):
        grads(name, sets[n], arrays, takes, gives)
        arrays["rows"] = arrays["rows_out"]
        arrays["dq_in"], arrays["dq_rest_in"] = arrays["dq"], arrays["dq_rest"]
        takes, gives = ["rows", "dq_in", "dq_rest_in"], ["dq", "dq_rest", "dkv_send"]
        sent[n] = shifted(arrays["dkv_send"], by)
        if n == 1:
            arrays["relay"] = sent[2]
            takes = [*takes, "relay"]
    arrays["prob_grad"] = prob_grad
    takes = ["rows", "dq_in", "dq_rest_in", "prob_grad"]
    gives = ["dq_send", "dq_rest", "dkv_out"]
    grads("grads_own_far", sets[0], arrays, takes, gives, blocks=(1,))
    far_dq = crossed(arrays["dq_send"])
    arrays["dkv_in"], arrays["dq_rest_in"] = arrays["dkv_out"], arrays["dq_rest"]
    sent[1], arrays["dq_in"] = lax.optimization_barrier((sent[1], arrays["dq_in"]))
    grads(
        "grads_own", sets[0], arrays, [*takes, "dkv_in"], ["dq_out", "dkv_out"], (0,), False
    )
    merged = call(
        merge_kernel,
        "merge",
        [shape(16, 128, 128)],
        [at, arrays["dq_out"], far_dq, arrays["dkv_out"], sent[1], sent[3]],
        smem_in=1,
        scratch=[pltpu.VMEM((OWN, 128), F32), pltpu.VMEM((OWN, 128), F32)],
    )[0]
    merged = lax.all_to_all(merged, BY_HEAD, 0, 0, tiled=True)
    return tuple(call(join_kernel, "join", [shape(ROWS, HEADS * HD)] * 3, [merged]))


def solution(mesh):
    fine = Mesh(mesh.devices.reshape(4, 2, 2, 2, 4), BLK + ("zh", "x"))
    rows = P(BLK + ("zh", "x"), None)
    return jax.shard_map(
        body,
        mesh=fine,
        in_specs=(rows, rows, rows, rows, P(BLK)),
        out_specs=(rows, rows, rows),
        check_vma=False,
    )
```
